512 devices in a mesh: gx: 64 (over z, x, core), gy: 8 (over y).
Axes of the slice: x: 4, y: 8, z: 8, core: 2. Of those that a mesh axis runs over, the one named last changes fastest.
Arguments:
- field: bfloat16 [16, 256, 192, 512], P(None, 'gx', 'gy'), may hold values from -6 to 6
- pointwise: bfloat16 [16, 16], replicated, may hold values from -1.5 to 1.5
- spectral: float32 [2304, 2, 16, 16, 32], P('gx', None, None, None, 'gy'), may hold values from -1 to 1
- momentum: float32 [2304, 2, 16, 16, 32], P('gx', None, None, None, 'gy'), may hold values from -6 to 6
- cotangent: bfloat16 [16, 256, 192, 512], P(None, 'gx', 'gy'), may hold values from -6 to 6
Outputs:
- momentum_next: float32 [2304, 2, 16, 16, 32], P('gx', None, None, None, 'gy')
The draws below stay inside these ranges and needn't reach their ends.
All inputs are finite; a program needn't handle non-finite values.
Results may differ from the reference program's by a relative error of at most 0.0025.
Values may be sent and summed in bfloat16 or wider, within the bound.
No kernel may reach another device: no remote copies, remote signals or barrier semaphores. Data moves between devices by JAX's collectives and lax.ppermute only.
A program may use at most 64 MiB of HBM per device.

```python
import math
import jax
import jax.numpy as jnp
from jax import lax

C = 16
MX = 48
MY = 48
MZ = 32
NZ = 512
NX = 256
NY = 192


def steps_of(own_key, dims, pieces, low, top_value):
    factor_of = 1.0
    for dim, parts in pieces:
        draws = jax.random.uniform(jax.random.fold_in(jax.random.fold_in(own_key, 6), dim), (parts,), jnp.float32, low / len(pieces), top_value / len(pieces))
        factor_of = factor_of * jnp.repeat(jnp.exp(draws), dims[dim] // parts).reshape((-1,) + (1,) * (len(dims) - 1 - dim))
    return factor_of


def normal_values(own_key, shape, deviation, reach, pieces=(), kind=jnp.bfloat16):
    loudness = steps_of(own_key, shape, pieces, -0.22, 0.18) if pieces else 1.0
    values = jax.random.normal(own_key, shape, jnp.float32) * deviation * loudness
    return jnp.minimum(jnp.maximum(values, -reach), reach).astype(kind)


def setup_inputs(seed: int = 0) -> dict:
    streams_of = jax.random.split(jax.random.key(seed), 6)
    field = normal_values(streams_of[0], (C, NX, NY, NZ), 1.0, 6.0, ((1, 64), (2, 8)))
    pointwise = normal_values(streams_of[1], (C, C), C ** -0.5, 1.5)
    spectral = normal_values(streams_of[2], (MX * MY, 2, C, C, MZ), (2 * C) ** -0.5, 1.0, ((0, 64), (4, 8)), jnp.float32)
    momentum = normal_values(streams_of[3], (MX * MY, 2, C, C, MZ), 1.0, 6.0, ((0, 64), (4, 8)), jnp.float32)
    cotangent = normal_values(streams_of[4], (C, NX, NY, NZ), 1.0, 6.0, ((1, 64), (2, 8)))
    return dict(field=field, pointwise=pointwise, spectral=spectral, momentum=momentum, cotangent=cotangent)


HIGH = lax.Precision.HIGHEST

def phase(first, second, length):
    return 2.0 * math.pi / length * (first * second % length).astype(jnp.float32)

def gelu_slope(pre):
    inner = 0.7978845608 * (pre + 0.044715 * pre * pre * pre)
    tanh_inner = jnp.tanh(inner)
    return 0.5 * (1.0 + tanh_inner) + 0.5 * pre * (1.0 - tanh_inner * tanh_inner) * 0.7978845608 * (1.0 + 3.0 * 0.044715 * pre * pre)

def z_forward(field):
    depth = field.shape[-1]
    zpos = lax.broadcasted_iota(jnp.int32, (depth, MZ), 0)
    kpos = lax.broadcasted_iota(jnp.int32, (depth, MZ), 1)
    angle = phase(zpos, kpos, depth)
    table = jnp.concatenate([jnp.cos(angle), -jnp.sin(angle)], axis=1).astype(jnp.bfloat16)
    flat = jnp.dot(field.reshape(-1, depth), table, preferred_element_type=jnp.float32)
    scaled = (flat / math.sqrt(depth)).astype(jnp.bfloat16)
    return scaled.reshape(field.shape[:-1] + (2, MZ))

def from_zmodes(zmodes):
    ypos = jnp.arange(NY, dtype=jnp.int32)
    kys = jnp.arange(MY, dtype=jnp.int32)
    angle_y = phase(ypos[:, None], kys[None, :], NY)
    cos_y = jnp.cos(angle_y) / math.sqrt(NY)
    sin_y = jnp.sin(angle_y) / math.sqrt(NY)
    real_in = zmodes[:, :, :, 0, :].astype(jnp.float32)
    imag_in = zmodes[:, :, :, 1, :].astype(jnp.float32)
    form = 'cxyk,yq->xqck'
    real_y = jnp.einsum(form, real_in, cos_y, precision=HIGH) + jnp.einsum(form, imag_in, sin_y, precision=HIGH)
    imag_y = jnp.einsum(form, imag_in, cos_y, precision=HIGH) - jnp.einsum(form, real_in, sin_y, precision=HIGH)
    xpos = jnp.arange(NX, dtype=jnp.int32)
    kxs = jnp.arange(MX, dtype=jnp.int32)
    angle_x = phase(xpos[:, None], kxs[None, :], NX)
    cos_x = jnp.cos(angle_x) / math.sqrt(NX)
    sin_x = jnp.sin(angle_x) / math.sqrt(NX)
    form = 'xqck,xp->pqck'
    real_x = jnp.einsum(form, real_y, cos_x, precision=HIGH) + jnp.einsum(form, imag_y, sin_x, precision=HIGH)
    imag_x = jnp.einsum(form, imag_y, cos_x, precision=HIGH) - jnp.einsum(form, real_y, sin_x, precision=HIGH)
    return (real_x.reshape(MX * MY, C, MZ), imag_x.reshape(MX * MY, C, MZ))

def reference(field, pointwise, spectral, momentum, cotangent):
    fwd_r, fwd_i = from_zmodes(z_forward(field))
    real_w = spectral[:, 0]
    imag_w = spectral[:, 1]
    form = 'qcok,qck->qok'
    mixed_r = jnp.einsum(form, real_w, fwd_r, precision=HIGH) - jnp.einsum(form, imag_w, fwd_i, precision=HIGH)
    mixed_i = jnp.einsum(form, real_w, fwd_i, precision=HIGH) + jnp.einsum(form, imag_w, fwd_r, precision=HIGH)
    mixed = jnp.stack([mixed_r, mixed_i], 1).astype(jnp.bfloat16)
    values = mixed.astype(jnp.float32).reshape(MX, MY, 2, C, MZ)
    kxs = jnp.arange(MX, dtype=jnp.int32)
    xpos = jnp.arange(NX, dtype=jnp.int32)
    angle_x = phase(kxs[:, None], xpos[None, :], NX)
    cos_x = jnp.cos(angle_x)
    sin_x = jnp.sin(angle_x)
    form = 'pqck,px->xqck'
    back_r = jnp.einsum(form, values[:, :, 0], cos_x, precision=HIGH) - jnp.einsum(form, values[:, :, 1], sin_x, precision=HIGH)
    back_i = jnp.einsum(form, values[:, :, 0], sin_x, precision=HIGH) + jnp.einsum(form, values[:, :, 1], cos_x, precision=HIGH)
    kys = jnp.arange(MY, dtype=jnp.int32)
    ypos = jnp.arange(NY, dtype=jnp.int32)
    angle_y = phase(kys[:, None], ypos[None, :], NY)
    factor = 1.0 / math.sqrt(MX * MY * MZ)
    cos_y = jnp.cos(angle_y) * factor
    sin_y = jnp.sin(angle_y) * factor
    form = 'xqck,qy->xyck'
    wave_r = jnp.einsum(form, back_r, cos_y, precision=HIGH) - jnp.einsum(form, back_i, sin_y, precision=HIGH)
    wave_i = jnp.einsum(form, back_r, sin_y, precision=HIGH) + jnp.einsum(form, back_i, cos_y, precision=HIGH)
    waves = jnp.stack([wave_r, wave_i], 2).astype(jnp.bfloat16)
    kzs = lax.broadcasted_iota(jnp.int32, (MZ, NZ), 0)
    zpos = lax.broadcasted_iota(jnp.int32, (MZ, NZ), 1)
    angle_z = phase(kzs, zpos, NZ)
    ztable = jnp.stack([jnp.cos(angle_z), -jnp.sin(angle_z)], 0).astype(jnp.bfloat16).astype(jnp.float32)
    weights_pw = pointwise.astype(jnp.float32)

    def row_step(items):
        wave_row, field_row, cot_row = items
        spec_out = jnp.einsum('yrck,rkz->cyz', wave_row.astype(jnp.float32), ztable, precision=HIGH)
        pre = spec_out + jnp.einsum('co,cyz->oyz', weights_pw, field_row.astype(jnp.float32), precision=HIGH)
        grad_pre = (cot_row.astype(jnp.float32) * gelu_slope(pre)).astype(jnp.bfloat16)
        return z_forward(grad_pre)
    rows = lax.map(row_step, (waves, jnp.moveaxis(field, 1, 0), jnp.moveaxis(cotangent, 1, 0)))
    grad_r, grad_i = from_zmodes(jnp.moveaxis(rows, 0, 1))
    d_real = grad_r[:, None] * fwd_r[:, :, None] + grad_i[:, None] * fwd_i[:, :, None]
    d_imag = grad_i[:, None] * fwd_r[:, :, None] - grad_r[:, None] * fwd_i[:, :, None]
    total = jnp.stack([d_real, d_imag], 1) + 2.0 * C * spectral
    return momentum - 0.25 * total
```

```python
import functools
import math

import jax
import jax.numpy as jnp
import ml_dtypes
import numpy as np
from jax import lax
from jax.experimental import pallas as pl
from jax.experimental.pallas import tpu as pltpu
from jax.sharding import PartitionSpec as P

C = 16
MX = 48
MY = 48
MZ = 32
NX = 256
NY = 192
NZ = 512
GX = 64
GY = 8
XL = NX // GX
YL = NY // GY
KZL = MZ // GY
ROWS = XL * YL
BF = jnp.bfloat16
F32 = jnp.float32
LANES = 128
CH2 = 24
CH6 = 40


def angle(a, b, n):
    return (2.0 * np.pi / n) * ((np.asarray(a)[:, None] * np.asarray(b)[None, :]) % n).astype(np.float64)


def split(table):
    table = np.asarray(table, np.float64)
    high = table.astype(ml_dtypes.bfloat16)
    low = (table - high.astype(np.float64)).astype(ml_dtypes.bfloat16)
    return high, low


def z_tables():
    a = angle(np.arange(NZ), np.arange(MZ), NZ).astype(np.float32)
    tab = np.stack([np.cos(a), -np.sin(a)], 0).astype(ml_dtypes.bfloat16)
    tab = tab.reshape(2, NZ, GY, KZL)
    fwd = np.zeros((2, NZ, 2, 2, GY, KZL), ml_dtypes.bfloat16)
    inv = np.zeros((2, 2, GY, KZL, 2, NZ), ml_dtypes.bfloat16)
    for h in range(2):
        fwd[h, :, :, h] = np.transpose(tab, (1, 0, 2, 3))
        inv[:, h, :, :, h, :] = np.transpose(tab, (0, 2, 3, 1))
    return fwd.reshape(2 * NZ, LANES), inv.reshape(LANES, 2 * NZ)


def y_forward_table():
    a = angle(np.arange(MY), np.arange(NY), NY)
    ch, cl = split(np.cos(a) / math.sqrt(NY))
    sh, sl = split(np.sin(a) / math.sqrt(NY))
    return np.concatenate([ch, cl, sh, sl], 0)


def x_forward_table():
    a = angle(np.arange(MX), np.arange(NX), NX)
    parts = []
    for t in split(np.cos(a) / math.sqrt(NX)) + split(np.sin(a) / math.sqrt(NX)):
        t = t.reshape(MX, GX, 1, XL)
        parts.append(np.concatenate([t, t], 2).reshape(MX, GX * 2 * XL))
    return np.concatenate(parts, 0)


def x_inverse_table():
    a = angle(np.arange(NX), np.arange(MX), NX)
    t = np.concatenate(split(np.cos(a)) + split(np.sin(a)), 1)
    out = np.zeros((GX, 8, 4 * MX), ml_dtypes.bfloat16)
    out[:, :XL] = t.reshape(GX, XL, 4 * MX)
    return out.reshape(GX * 8, 4 * MX)


def y_inverse_table():
    a = angle(np.arange(NY), np.arange(MY), NY)
    factor = 1.0 / math.sqrt(MX * MY * MZ)
    return np.concatenate(split(np.cos(a) * factor) + split(np.sin(a) * factor), 1)


def expand_table():
    e = np.zeros((2, C, KZL, 8, 2, 2, C, KZL), ml_dtypes.bfloat16)
    for r in range(2):
        for c in range(C):
            for k in range(KZL):
                e[r, c, k, c // 2, r, c % 2, :, k] = 1.0
    return e.reshape(LANES, 8 * 2 * LANES)


def dot(a, b):
    return jnp.dot(a, b, preferred_element_type=F32)


def dot_t(a, b, **kw):
    return lax.dot_general(a, b, (((1,), (1,)), ((), ())), preferred_element_type=F32, **kw)


def lane_of(shape):
    return lax.broadcasted_iota(jnp.int32, shape, len(shape) - 1)


def exchange_groups(arrays):
    arrays = list(arrays)
    lane = lane_of(arrays[0].shape)
    for bit in range(3):
        stride = 4 << bit
        clear = (lane & stride) == 0
        for i in range(8):
            if i & (1 << bit):
                continue
            lo, hi = arrays[i], arrays[i | (1 << bit)]
            arrays[i] = jnp.where(clear, lo, pltpu.roll(hi, stride, 1))
            arrays[i | (1 << bit)] = jnp.where(clear, pltpu.roll(lo, LANES - stride, 1), hi)
    return arrays


def times_minus_i(v):
    return pltpu.roll(v, 64, 1) * jnp.where(lane_of(v.shape) < 64, 1.0, -1.0)


def times_plus_i(v):
    return pltpu.roll(v, 64, 1) * jnp.where(lane_of(v.shape) < 64, -1.0, 1.0)


def write_z_modes(even, odd, w_ref, out_ref):
    modes = dot(even, w_ref[0:NZ, :]) + dot(odd, w_ref[NZ : 2 * NZ, :])
    modes = modes / math.sqrt(NZ)
    parts = exchange_groups([modes[16 * i : 16 * i + 16] for i in range(8)])
    for p in range(GY):
        out_ref[p] = parts[p].astype(BF)


def k1(field_ref, w_ref, out_ref):
    x = field_ref[...].reshape(C * 16, NZ)
    write_z_modes(x[0:128], x[128:256], w_ref, out_ref)


def y_transform(in_ref, ty_ref):
    full = in_ref[...].astype(F32)
    out = []
    for x in range(XL):
        rows = jnp.concatenate([full[p, YL * x : YL * x + YL, :] for p in range(GY)], 0).astype(BF)
        t = dot(ty_ref[...], rows)
        cos, sin = t[0:48] + t[48:96], t[96:144] + t[144:192]
        out.append(cos + times_minus_i(sin))
    return out


def k2(in_ref, spec_ref, ty_ref, out_ref, scratch):
    quarter = lax.axis_index("gx") % 4
    j = lax.broadcasted_iota(jnp.int32, (MY, 36), 0)
    t = lax.broadcasted_iota(jnp.int32, (MY, 36), 1) + 36 * quarter
    t = t - jnp.where(t >= 48, 48, 0) - jnp.where(t >= 96, 48, 0)
    select = (t == j).astype(BF)
    for k in range(16):
        block = spec_ref[128 * k : 128 * k + 128, :].astype(BF)
        scratch[pl.ds(k, MY, stride=CH2), :] = dot_t(select, block)
    for x, v in enumerate(y_transform(in_ref, ty_ref)):
        high = v.astype(BF).astype(F32)
        scratch[pl.ds(16 + x, MY, stride=CH2), :] = high
        scratch[pl.ds(20 + x, MY, stride=CH2), :] = v - high
    out_ref[0 : MY * CH2, :] = scratch[...].astype(BF)
    out_ref[MY * CH2 : GX * CH2, :] = jnp.zeros(((GX - MY) * CH2, LANES), BF)


def k3(in_ref, tx_ref, e_ref, tinv_ref, out_ref, scratch):
    ky = lax.axis_index("gx")
    data = in_ref[:, 16:24, :].astype(F32).reshape(GX * 8, LANES).astype(BF)
    t = dot(tx_ref[...], data)
    fwd = t[0:48] + t[48:96] + times_minus_i(t[96:144] + t[144:192])
    high = fwd.astype(BF)
    low = (fwd - high.astype(F32)).astype(BF)
    both = jnp.concatenate([high, low], 0)
    source = (
        jnp.where(ky >= 36, 1, 0),
        1 + jnp.where(ky >= 24, 1, 0),
        2 + jnp.where(ky >= 12, 1, 0),
    )
    for kx in range(MX):
        block = in_ref[4 * (kx // 3) + source[kx % 3], 0:16, :]
        scratch[16 * kx : 16 * kx + 16, :] = block.astype(F32)
    mixed_r = jnp.zeros((MX, LANES), F32)
    mixed_i = jnp.zeros((MX, LANES), F32)
    for k in range(8):
        wide = dot(both, e_ref[:, 256 * k : 256 * k + 256])
        wide = wide[0:48] + wide[48:96]
        fr, fi = wide[:, 0:128], wide[:, 128:256]
        wr = scratch[pl.ds(k, MX, stride=16), :]
        wi = scratch[pl.ds(8 + k, MX, stride=16), :]
        mixed_r += wr * fr - wi * fi
        mixed_i += wr * fi + wi * fr
    mixed_r += pltpu.roll(mixed_r, 64, 1)
    mixed_i += pltpu.roll(mixed_i, 64, 1)
    mixed = jnp.where(lane_of(mixed_r.shape) < 64, mixed_r, mixed_i)
    mixed = mixed.astype(BF)
    turned = times_plus_i(mixed.astype(F32)).astype(BF)
    row = lax.broadcasted_iota(jnp.int32, (GX * 8, 2 * MX), 0)
    col = lax.broadcasted_iota(jnp.int32, (GX * 8, 2 * MX), 1)
    owner = row // 8
    part = row % 8
    quarter = owner % 4
    back_one = jnp.where(quarter == 1, jnp.where(ky >= 36, 1, 0), 0)
    back_one += jnp.where(quarter == 2, jnp.where(ky >= 24, 1, 0), 0)
    kx_of = 3 * (owner // 4) + jnp.minimum(quarter, 2) - back_one
    wanted = jnp.where(part == 4, kx_of, jnp.where(part == 5, kx_of + MX, -1))
    select = (col == wanted).astype(BF)
    result = dot(tinv_ref[...], jnp.concatenate([mixed, mixed, turned, turned], 0))
    result += dot(select, both)
    out_ref[...] = result.astype(BF)


def k4(in_ref, ty_ref, out_ref, scratch):
    scratch[...] = in_ref[0 : 8 * MY, :].astype(F32)
    for x in range(XL):
        v = scratch[pl.ds(x, MY, stride=8), :]
        b = v.astype(BF)
        s = times_plus_i(v).astype(BF)
        w = dot(ty_ref[...], jnp.concatenate([b, b, s, s], 0))
        for p in range(GY):
            out_ref[p, YL * x : YL * x + YL, :] = w[YL * p : YL * p + YL].astype(BF)


def slope(pre):
    inner = 0.7978845608 * (pre + 0.044715 * pre * pre * pre)
    t = jnp.tanh(inner)
    return 0.5 * (1.0 + t) + 0.5 * pre * (1.0 - t * t) * 0.7978845608 * (1.0 + 3.0 * 0.044715 * pre * pre)


def k5(waves_ref, field_ref, cot_ref, pw_ref, w_ref, zt_ref, out_ref, kron):
    @pl.when(pl.program_id(0) == 0)
    def _():
        group = lax.broadcasted_iota(jnp.int32, (256, C), 0) // 16
        member = lax.broadcasted_iota(jnp.int32, (256, C), 1)
        one_hot = (group == member).astype(BF)
        wide = dot_t(one_hot, pw_ref[...]).astype(BF)
        wide = dot_t(wide, one_hot)
        r = lax.broadcasted_iota(jnp.int32, (256, 256), 0) % 16
        s = lax.broadcasted_iota(jnp.int32, (256, 256), 1) % 16
        kron[...] = jnp.where(r == s, wide, 0.0).astype(BF)

    groups = exchange_groups([waves_ref[p].astype(F32) for p in range(GY)])
    waves = jnp.concatenate(groups, 0).astype(BF)
    x = field_ref[...].reshape(C * 16, NZ)
    halves = []
    for h in range(2):
        pre = dot(waves, zt_ref[:, NZ * h : NZ * h + NZ])
        pre += dot(kron[128 * h : 128 * h + 128, :], x)
        cot = cot_ref[8 * h : 8 * h + 8].reshape(128, NZ).astype(F32)
        halves.append((cot * slope(pre)).astype(BF))
    write_z_modes(halves[0], halves[1], w_ref, out_ref)


def k6(in_ref, ty_ref, cs_ref, out_ref):
    base = XL * lax.axis_index("gx")
    values = y_transform(in_ref, ty_ref)
    turned = [times_minus_i(v) for v in values]

    def body(g, carry):
        rows = []
        for r in range(3):
            kx = 3 * g + r
            acc = None
            for x in range(XL):
                at = (kx * (base + x)) & (NX - 1)
                term = values[x] * cs_ref[at] + turned[x] * cs_ref[NX + at]
                acc = term if acc is None else acc + term
            rows.append(acc)
        a, b, c = rows
        out_ref[4 * g] = a[0:40].astype(BF)
        out_ref[4 * g + 1] = jnp.concatenate([b[0:24], a[32:48]], 0).astype(BF)
        out_ref[4 * g + 2] = jnp.concatenate([b[24:48], c[0:16]], 0).astype(BF)
        out_ref[4 * g + 3] = c[8:48].astype(BF)
        return carry

    lax.fori_loop(0, MX // 3, body, 0)


def k7(in_ref, fwd_ref, spec_ref, mom_ref, out_ref):
    quarter = lax.axis_index("gx") % 4
    total = in_ref[0].astype(F32)
    for g in range(1, GX):
        total += in_ref[g].astype(F32)
    to = lax.broadcasted_iota(jnp.int32, (LANES, CH6), 0)
    at = lax.broadcasted_iota(jnp.int32, (LANES, CH6), 1)
    source = jnp.where(
        quarter == 1,
        jnp.where(to < 12, to + 28, to - 12),
        jnp.where(quarter == 3, to + 4, to),
    )
    source = jnp.where(to < 36, source, -1)
    select = (at == source).astype(F32)
    grads = jnp.dot(select, total, precision=lax.Precision.HIGHEST, preferred_element_type=F32)
    to = lax.broadcasted_iota(jnp.int32, (LANES, 8 * MY), 0)
    at = lax.broadcasted_iota(jnp.int32, (LANES, 8 * MY), 1)
    t = to + 36 * quarter
    t = t - jnp.where(t >= 48, 48, 0) - jnp.where(t >= 96, 48, 0)
    hit = ((at // 8) == t) & ((at % 8) >= 4) & ((at % 8) < 6) & (to < 36)
    fwd = dot(hit.astype(BF), fwd_ref[0 : 8 * MY, :])
    grads = grads.T[:, 0:36]
    fwd = fwd.T[:, 0:36]
    grad_r, grad_i = grads[0:64], grads[64:128]
    for c in range(C):
        fr = fwd[4 * c : 4 * c + 4]
        fi = fwd[64 + 4 * c : 68 + 4 * c]
        fr = jnp.concatenate([fr] * 16, 0)
        fi = jnp.concatenate([fi] * 16, 0)
        d_real = grad_r * fr + grad_i * fi
        d_imag = grad_i * fr - grad_r * fi
        out_ref[0, c] = mom_ref[0, c] - 0.25 * (d_real + 2.0 * C * spec_ref[0, c])
        out_ref[1, c] = mom_ref[1, c] - 0.25 * (d_imag + 2.0 * C * spec_ref[1, c])


def call(body, out, *args, scratch=(), smem=()):
    specs = [
        pl.BlockSpec(memory_space=pltpu.SMEM if i in smem else pltpu.VMEM) for i in range(len(args))
    ]
    return pl.pallas_call(
        body,
        out_shape=out,
        in_specs=specs,
        out_specs=pl.BlockSpec(memory_space=pltpu.VMEM),
        scratch_shapes=list(scratch),
        compiler_params=pltpu.CompilerParams(vmem_limit_bytes=40 * 1024 * 1024),
    )(*args)


def whole(shape):
    return pl.BlockSpec(shape, lambda i: (0,) * len(shape))


def swap(value, axis):
    return lax.all_to_all(value, axis, split_axis=0, concat_axis=0, tiled=True)


def on_device(field, pointwise, spectral, momentum, cotangent):
    field = field.reshape(C, ROWS, NZ)
    cotangent = cotangent.reshape(C, ROWS, NZ)
    spectral = jnp.transpose(spectral, (1, 2, 3, 4, 0))
    momentum = jnp.transpose(momentum, (1, 2, 3, 4, 0))
    zf, zi = z_tables()
    zf, zi = jnp.asarray(zf), jnp.asarray(zi)
    ty = jnp.asarray(y_forward_table())
    steps = ROWS // 16
    zshape = jax.ShapeDtypeStruct((GY, ROWS, LANES), BF)
    zblock = pl.BlockSpec((GY, 16, LANES), lambda i: (0, i, 0))
    fblock = pl.BlockSpec((C, 16, NZ), lambda i: (0, i, 0))
    zmodes = pl.pallas_call(
        k1,
        out_shape=zshape,
        grid=(steps,),
        in_specs=[fblock, whole((2 * NZ, LANES))],
        out_specs=zblock,
    )(field, zf)
    zmodes = swap(zmodes, "gy")
    sent = call(
        k2,
        jax.ShapeDtypeStruct((GX * CH2, LANES), BF),
        zmodes,
        spectral.reshape(2 * C * C * KZL, 36),
        ty,
        scratch=[pltpu.VMEM((MY * CH2, LANES), F32)],
    )
    got = swap(sent.reshape(GX, CH2, LANES), "gx")
    sent = call(
        k3,
        jax.ShapeDtypeStruct((GX * 8, LANES), BF),
        got,
        jnp.asarray(x_forward_table()),
        jnp.asarray(expand_table()),
        jnp.asarray(x_inverse_table()),
        scratch=[pltpu.VMEM((MX * 16, LANES), F32)],
    )
    back = swap(sent.reshape(GX, 8, LANES), "gx").reshape(GX * 8, LANES)
    waves = call(
        k4,
        zshape,
        back,
        jnp.asarray(y_inverse_table()),
        scratch=[pltpu.VMEM((8 * MY, LANES), F32)],
    )
    waves = swap(waves, "gy")
    zgrads = pl.pallas_call(
        k5,
        out_shape=zshape,
        grid=(steps,),
        in_specs=[
            zblock,
            fblock,
            fblock,
            whole((C, C)),
            whole((2 * NZ, LANES)),
            whole((LANES, 2 * NZ)),
        ],
        out_specs=zblock,
        scratch_shapes=[pltpu.VMEM((256, 256), BF)],
    )(waves, field, cotangent, pointwise, zf, zi)
    zgrads = swap(zgrads, "gy")
    turn = 2.0 * np.pi / NX * np.arange(NX)
    cs = np.concatenate([np.cos(turn), np.sin(turn)]) / math.sqrt(NX)
    partial = call(
        k6,
        jax.ShapeDtypeStruct((GX, CH6, LANES), BF),
        zgrads,
        ty,
        jnp.asarray(cs.astype(np.float32)),
        smem=(2,),
    )
    partial = swap(partial, "gx")
    result = call(
        k7,
        jax.ShapeDtypeStruct((2, C, C * KZL, 36), F32),
        partial,
        back,
        spectral.reshape(2, C, C * KZL, 36),
        momentum.reshape(2, C, C * KZL, 36),
    )
    result = result.reshape(2, C, C, KZL, 36)
    return jnp.transpose(result, (4, 0, 1, 2, 3))


def solution(mesh):
    in_specs = (
        P(None, "gx", "gy", None),
        P(),
        P("gx", None, None, None, "gy"),
        P("gx", None, None, None, "gy"),
        P(None, "gx", "gy", None),
    )
    out_specs = P("gx", None, None, None, "gy")
    return jax.shard_map(
        on_device, mesh=mesh, in_specs=in_specs, out_specs=out_specs, check_vma=False
    )
```

```python
import math

import jax
import jax.numpy as jnp
import ml_dtypes
import numpy as np
from jax import lax
from jax.experimental import pallas as pl
from jax.experimental.pallas import tpu as pltpu
from jax.sharding import PartitionSpec as P

C = 16
MX = 48
MY = 48
MZ = 32
NX = 256
NY = 192
NZ = 512
GX = 64
GY = 8
XL = NX // GX
YL = NY // GY
KZL = MZ // GY
ROWS = XL * YL
BF = jnp.bfloat16
F32 = jnp.float32
LANES = 128
OWNED = MX * MY // GX
TRIPLES = np.arange(48).reshape(16, 3).T.reshape(48)


def angle(a, b, n):
    return (2.0 * np.pi / n) * ((np.asarray(a)[:, None] * np.asarray(b)[None, :]) % n).astype(np.float64)


def split(table):
    table = np.asarray(table, np.float64)
    high = table.astype(ml_dtypes.bfloat16)
    low = (table - high.astype(np.float64)).astype(ml_dtypes.bfloat16)
    return high, low


def z_tables():
    a = angle(np.arange(NZ), np.arange(MZ), NZ).astype(np.float32)
    tab = np.stack([np.cos(a), -np.sin(a)], 0).astype(ml_dtypes.bfloat16)
    tab = tab.reshape(2, NZ, GY, KZL)
    mid = np.zeros((2, NZ, KZL, 2, 2, GY), ml_dtypes.bfloat16)
    own = np.zeros((2, NZ, 2, 2, GY, KZL), ml_dtypes.bfloat16)
    inv = np.zeros((KZL, 2, 2, GY, 2, NZ), ml_dtypes.bfloat16)
    for h in range(2):
        mid[h, :, :, :, h] = np.transpose(tab, (1, 3, 0, 2))
        own[h, :, :, h] = np.transpose(tab, (1, 0, 2, 3))
        inv[:, :, h, :, h, :] = np.transpose(tab, (3, 0, 2, 1))
    return mid.reshape(2 * NZ, LANES), own.reshape(2 * NZ, LANES), inv.reshape(LANES, 2 * NZ)


def y_forward_table(kys):
    a = angle(kys, np.arange(NY), NY)
    return np.concatenate(split(np.cos(a) / math.sqrt(NY)) + split(np.sin(a) / math.sqrt(NY)), 0)


def x_forward_table():
    xs = np.arange(NX).reshape(GX, XL).T.reshape(NX)
    a = angle(TRIPLES, xs, NX)
    return np.concatenate(split(np.cos(a) / math.sqrt(NX)) + split(np.sin(a) / math.sqrt(NX)), 0)


def x_inverse_table():
    a = angle(np.arange(NX), TRIPLES, NX)
    return np.concatenate(split(np.cos(a)) + split(np.sin(a)), 1)


def y_inverse_table():
    a = angle(np.arange(NY), TRIPLES, NY)
    factor = 1.0 / math.sqrt(MX * MY * MZ)
    return np.concatenate(split(np.cos(a) * factor) + split(np.sin(a) * factor), 1)


def expand_table():
    e = np.zeros((4, 2, 2, 8, 3, 2, 2, 8, C), ml_dtypes.bfloat16)
    for i in range(3):
        for r in range(2):
            for h in range(2):
                for c in range(8):
                    e[i, r, h, c, i, h, r, c, :] = 1.0
    return e.reshape(LANES, 6 * 2 * LANES)


def reorder_table():
    t = np.zeros((KZL, 2, C, 2, C, KZL), ml_dtypes.bfloat16)
    for k in range(KZL):
        for r in range(2):
            for c in range(C):
                t[k, r, c, r, c, k] = 1.0
    return t.reshape(LANES, LANES)


def dot(a, b):
    return jnp.dot(a, b, preferred_element_type=F32)


def dot_t(a, b):
    return lax.dot_general(a, b, (((1,), (1,)), ((), ())), preferred_element_type=F32)


def lane_of(shape):
    return lax.broadcasted_iota(jnp.int32, shape, len(shape) - 1)


def exchange(arrays, first):
    arrays = list(arrays)
    lane = lane_of(arrays[0].shape)
    bit = 1
    while bit < len(arrays):
        stride = first * bit
        clear = (lane & stride) == 0
        for i in range(len(arrays)):
            if i & bit:
                continue
            lo, hi = arrays[i], arrays[i | bit]
            arrays[i] = jnp.where(clear, lo, pltpu.roll(hi, stride, 1))
            arrays[i | bit] = jnp.where(clear, pltpu.roll(lo, LANES - stride, 1), hi)
        bit *= 2
    return arrays


def partner(v, stride):
    real = (lane_of(v.shape) & stride) == 0
    if stride == 64:
        return pltpu.roll(v, 64, 1), real
    return jnp.where(real, pltpu.roll(v, LANES - stride, 1), pltpu.roll(v, stride, 1)), real


def times_minus_i(v, stride):
    other, real = partner(v, stride)
    return jnp.where(real, other, -other)


def times_plus_i(v, stride):
    other, real = partner(v, stride)
    return jnp.where(real, -other, other)


def z_modes(even, odd, w_ref, first):
    modes = dot(even, w_ref[0:NZ, :]) + dot(odd, w_ref[NZ : 2 * NZ, :])
    modes = modes * (1.0 / math.sqrt(NZ))
    n = modes.shape[0] // 8
    return exchange([modes[n * i : n * i + n] for i in range(8)], first)


def k1(field_ref, w_ref, out_ref):
    even = field_ref[0:8].reshape(8 * ROWS, NZ)
    odd = field_ref[8:16].reshape(8 * ROWS, NZ)
    for p, v in enumerate(z_modes(even, odd, w_ref, 1)):
        out_ref[p] = v.astype(BF)


def y_transform(in_ref, ty_ref, stride):
    full = in_ref[...].astype(F32)
    out = []
    for x in range(XL):
        rows = jnp.concatenate([full[p, YL * x : YL * x + YL, :] for p in range(GY)], 0).astype(BF)
        t = dot(ty_ref[...], rows)
        cos, sin = t[0:48] + t[48:96], t[96:144] + t[144:192]
        out.append(cos + times_minus_i(sin, stride))
    return out


def ky_of(value, quarter):
    t = value + OWNED * quarter
    return t - jnp.where(t >= 48, 48, 0) - jnp.where(t >= 96, 48, 0)


def k2(in_ref, spec_ref, ty_ref, out_ref, scratch):
    quarter = lax.axis_index("gx") % 4
    row = lax.broadcasted_iota(jnp.int32, (MY, OWNED), 0)
    mode = ky_of(lax.broadcasted_iota(jnp.int32, (MY, OWNED), 1), quarter)
    select = (mode == 3 * (row % 16) + row // 16).astype(BF)
    for k in range(4):
        for b in range(KZL):
            block = spec_ref[pl.ds(512 * k + b, LANES, stride=KZL), :].astype(BF)
            moved = dot_t(select, block)
            for i in range(3):
                scratch[pl.ds(16 * b + 4 + 4 * i + k, 16, stride=64), :] = moved[16 * i : 16 * i + 16]
    for x, v in enumerate(y_transform(in_ref, ty_ref, 16)):
        parts = [v[0:16], v[16:32], v[32:48], jnp.zeros((16, LANES), F32)]
        for b, part in enumerate(exchange(parts, 32)):
            scratch[pl.ds(16 * b + x, 16, stride=64), :] = part
    out_ref[...] = scratch[...].astype(BF)


def k3(in_ref, tx_ref, e_ref, tinv_ref, out_ref, scratch):
    a = lax.axis_index("gx") // 4
    scratch[...] = in_ref[...].astype(F32)
    data = jnp.concatenate([scratch[pl.ds(x, GX, stride=16), :] for x in range(XL)], 0).astype(BF)
    t = dot(tx_ref[...], data)
    fwd = t[0:48] + t[48:96] + times_minus_i(t[96:144] + t[144:192], 16)
    high = fwd.astype(BF)
    low = (fwd - high.astype(F32)).astype(BF)
    both = jnp.concatenate([high, low], 0)
    source = (
        jnp.where(a >= 12, 1, 0),
        1 + jnp.where(a >= 8, 1, 0),
        2 + jnp.where(a >= 4, 1, 0),
    )

    def weights(i, k):
        at = 4 + 4 * i + k
        return jnp.concatenate(
            [scratch[pl.ds(16 * source[r] + at, 16, stride=64), :] for r in range(3)], 0
        )

    group = lane_of((MX, LANES)) // 16
    mixed = jnp.zeros((MX, LANES), F32)
    for i in range(3):
        sums = [0.0, 0.0]
        for h in range(2):
            at = 256 * (2 * i + h)
            wide = dot(both, e_ref[:, at : at + 256])
            wide = wide[0:48] + wide[48:96]
            fr, fi = wide[:, 0:128], wide[:, 128:256]
            wr, wi = weights(i, h), weights(i, 2 + h)
            sums[0] += wr * fr - wi * fi
            sums[1] += wr * fi + wi * fr
        for r in range(2):
            v = sums[r]
            for stride in (64, 32, 16):
                v = v + pltpu.roll(v, stride, 1)
            mixed = jnp.where(group == 2 * i + r, v, mixed)
    mixed = mixed.astype(BF)
    turned = times_plus_i(mixed.astype(F32), 16).astype(BF)
    moved = [
        jnp.where(group >= 6, pltpu.roll(high.astype(F32), 96 - 32 * i, 1), 0.0)
        for i in range(3)
    ]
    moved = jnp.concatenate(moved, 0).astype(BF)
    row = lax.broadcasted_iota(jnp.int32, (NX, 3 * MX), 0)
    col = lax.broadcasted_iota(jnp.int32, (NX, 3 * MX), 1)
    owner = row // 4
    quarter = owner % 4
    back_one = jnp.where(quarter == 1, jnp.where(a >= 12, 1, 0), 0)
    back_one += jnp.where(quarter == 2, jnp.where(a >= 8, 1, 0), 0)
    r = jnp.minimum(quarter, 2) - back_one
    wanted = MX * (row % 4) + 16 * r + owner // 4
    select = (col == wanted).astype(BF)
    result = dot(tinv_ref[...], jnp.concatenate([mixed, mixed, turned, turned], 0))
    result += dot(select, moved)
    out_ref[...] = result.astype(BF)


def k4(in_ref, ty_ref, out_ref, fwd_ref, scratch):
    scratch[...] = in_ref[...].astype(F32)
    for x in range(XL):
        parts = [scratch[pl.ds(4 * b + x, 16, stride=16), :] for b in range(KZL)]
        parts = exchange(parts, 32)
        if x < 3:
            fwd_ref[16 * x : 16 * x + 16, :] = parts[3]
        v = jnp.concatenate(parts[0:3], 0)
        b = v.astype(BF)
        s = times_plus_i(v, 16).astype(BF)
        w = dot(ty_ref[...], jnp.concatenate([b, b, s, s], 0))
        for p in range(GY):
            out_ref[p, YL * x : YL * x + YL, :] = w[YL * p : YL * p + YL].astype(BF)


def slope(pre):
    square = pre * pre
    t = jnp.tanh(pre * (0.7978845608 + 0.7978845608 * 0.044715 * square))
    ramp = pre * (0.5 * 0.7978845608 + 1.5 * 0.7978845608 * 0.044715 * square)
    return (0.5 + 0.5 * t) + (1.0 - t * t) * ramp


def k5(waves_ref, field_ref, cot_ref, pw_ref, w_ref, zt_ref, out_ref, kron, grad):
    group = lax.broadcasted_iota(jnp.int32, (256, C), 0) // 16
    member = lax.broadcasted_iota(jnp.int32, (256, C), 1)
    one_hot = (group == member).astype(BF)
    wide = dot_t(dot_t(one_hot, pw_ref[...]).astype(BF), one_hot)
    r = lax.broadcasted_iota(jnp.int32, (256, 256), 0) % 16
    s = lax.broadcasted_iota(jnp.int32, (256, 256), 1) % 16
    kron[...] = jnp.where(r == s, wide, 0.0).astype(BF)
    for n in range(ROWS // 16):
        rows = slice(16 * n, 16 * n + 16)
        parts = exchange([waves_ref[p, rows, :].astype(F32) for p in range(GY)], 1)
        waves = jnp.concatenate(parts, 0).astype(BF)
        x = field_ref[:, rows, :].reshape(C * 16, NZ)
        for h in range(2):
            pre = dot(waves, zt_ref[:, NZ * h : NZ * h + NZ])
            pre += dot(kron[128 * h : 128 * h + 128, :], x)
            cot = cot_ref[8 * h : 8 * h + 8, rows, :].reshape(128, NZ).astype(F32)
            grad[8 * h : 8 * h + 8, rows, :] = (cot * slope(pre)).astype(BF).reshape(8, 16, NZ)
    even = grad[0:8].reshape(8 * ROWS, NZ)
    odd = grad[8:16].reshape(8 * ROWS, NZ)
    for p, v in enumerate(z_modes(even, odd, w_ref, 4)):
        out_ref[p] = v.astype(BF)


def k6(in_ref, ty_ref, cs_ref, out_ref):
    base = XL * lax.axis_index("gx")
    values = y_transform(in_ref, ty_ref, 64)
    turned = [times_minus_i(v, 64) for v in values]

    def body(g, carry):
        for r in range(3):
            kx = 3 * g + r
            acc = None
            for x in range(XL):
                at = (kx * (base + x)) & (NX - 1)
                term = values[x] * cs_ref[at] + turned[x] * cs_ref[NX + at]
                acc = term if acc is None else acc + term
            out_ref[pl.ds(pl.multiple_of(48 * kx, 16), 48), :] = acc.astype(BF)
        return carry

    lax.fori_loop(0, MX // 3, body, 0)


def k7(in_ref, fwd_ref, reorder_ref, spec_ref, mom_ref, out_ref, scratch):
    quarter = lax.axis_index("gx") % 4
    pair = 2 * OWNED
    total = in_ref[0:pair, :].astype(F32)
    for g in range(1, GX // 2):
        total += in_ref[pair * g : pair * g + pair, :].astype(F32)
    scratch[0:pair, :] = total
    scratch[pair : pair + 8, :] = jnp.zeros((8, LANES), F32)
    grads = scratch[0:40, :] + scratch[OWNED : OWNED + 40, :]
    grads = jnp.concatenate([grads, jnp.zeros((LANES - 40, LANES), F32)], 0)
    row = lax.broadcasted_iota(jnp.int32, (LANES, MY), 0)
    col = lax.broadcasted_iota(jnp.int32, (LANES, MY), 1)
    hit = (ky_of(row, quarter) == 3 * (col % 16) + col // 16) & (row < OWNED)
    fwd = dot(hit.astype(BF), fwd_ref[...].astype(BF)).astype(BF)
    fwd = dot(fwd, reorder_ref[...])
    grads = grads.T[:, 0:OWNED]
    fwd = fwd.T[:, 0:OWNED]
    grad_r, grad_i = grads[0:64], grads[64:128]
    for c in range(C):
        fr = fwd[4 * c : 4 * c + 4]
        fi = fwd[64 + 4 * c : 68 + 4 * c]
        fr = jnp.concatenate([fr] * 16, 0)
        fi = jnp.concatenate([fi] * 16, 0)
        d_real = grad_r * fr + grad_i * fi
        d_imag = grad_i * fr - grad_r * fi
        out_ref[0, c] = mom_ref[0, c] - 0.25 * (d_real + 2.0 * C * spec_ref[0, c])
        out_ref[1, c] = mom_ref[1, c] - 0.25 * (d_imag + 2.0 * C * spec_ref[1, c])


def call(body, out, *args, scratch=(), smem=()):
    specs = [
        pl.BlockSpec(memory_space=pltpu.SMEM if i in smem else pltpu.VMEM) for i in range(len(args))
    ]
    vmem = pl.BlockSpec(memory_space=pltpu.VMEM)
    return pl.pallas_call(
        body,
        out_shape=out,
        in_specs=specs,
        out_specs=jax.tree.map(lambda _: vmem, out),
        scratch_shapes=list(scratch),
        compiler_params=pltpu.CompilerParams(vmem_limit_bytes=40 * 1024 * 1024),
    )(*args)


def swap(value, axis):
    return lax.all_to_all(value, axis, split_axis=0, concat_axis=0, tiled=True)


def on_device(field, pointwise, spectral, momentum, cotangent):
    field = field.reshape(C, ROWS, NZ)
    cotangent = cotangent.reshape(C, ROWS, NZ)
    spectral = jnp.transpose(spectral, (1, 2, 3, 4, 0))
    momentum = jnp.transpose(momentum, (1, 2, 3, 4, 0))
    z_mid, z_own, z_inv = [jnp.asarray(t) for t in z_tables()]
    zshape = jax.ShapeDtypeStruct((GY, ROWS, LANES), BF)

    zmodes = swap(call(k1, zshape, field, z_mid), "gy")
    sent = call(
        k2,
        jax.ShapeDtypeStruct((GX * 16, LANES), BF),
        zmodes,
        spectral.reshape(2 * C * C * KZL, OWNED),
        jnp.asarray(y_forward_table(TRIPLES)),
        scratch=[pltpu.VMEM((GX * 16, LANES), F32)],
    )
    got = swap(sent.reshape(GX, 16, LANES), "gx").reshape(GX * 16, LANES)
    sent = call(
        k3,
        jax.ShapeDtypeStruct((NX, LANES), BF),
        got,
        jnp.asarray(x_forward_table()),
        jnp.asarray(expand_table()),
        jnp.asarray(x_inverse_table()),
        scratch=[pltpu.VMEM((GX * 16, LANES), F32)],
    )
    back = swap(sent.reshape(GX, XL, LANES), "gx").reshape(NX, LANES)
    waves, fwd = call(
        k4,
        (zshape, jax.ShapeDtypeStruct((MY, LANES), F32)),
        back,
        jnp.asarray(y_inverse_table()),
        scratch=[pltpu.VMEM((NX, LANES), F32)],
    )
    zgrads = call(
        k5,
        zshape,
        swap(waves, "gy"),
        field,
        cotangent,
        pointwise,
        z_own,
        z_inv,
        scratch=[pltpu.VMEM((256, 256), BF), pltpu.VMEM((C, ROWS, NZ), BF)],
    )
    turn = 2.0 * np.pi / NX * np.arange(NX)
    cs = np.concatenate([np.cos(turn), np.sin(turn)]) / math.sqrt(NX)
    partial = call(
        k6,
        jax.ShapeDtypeStruct((MX * MY, LANES), BF),
        swap(zgrads, "gy"),
        jnp.asarray(y_forward_table(np.arange(MY))),
        jnp.asarray(cs.astype(np.float32)),
        smem=(2,),
    )
    partial = swap(partial.reshape(GX, OWNED // 4, 4, LANES), "gx").reshape(MX * MY, LANES)
    result = call(
        k7,
        jax.ShapeDtypeStruct((2, C, C * KZL, OWNED), F32),
        partial,
        fwd,
        jnp.asarray(reorder_table()),
        spectral.reshape(2, C, C * KZL, OWNED),
        momentum.reshape(2, C, C * KZL, OWNED),
        scratch=[pltpu.VMEM((2 * OWNED + 8, LANES), F32)],
    )
    result = result.reshape(2, C, C, KZL, OWNED)
    return jnp.transpose(result, (4, 0, 1, 2, 3))


def solution(mesh):
    in_specs = (
        P(None, "gx", "gy", None),
        P(),
        P("gx", None, None, None, "gy"),
        P("gx", None, None, None, "gy"),
        P(None, "gx", "gy", None),
    )
    out_specs = P("gx", None, None, None, "gy")
    return jax.shard_map(
        on_device, mesh=mesh, in_specs=in_specs, out_specs=out_specs, check_vma=False
    )
```

```python
import math

import jax
import jax.numpy as jnp
import ml_dtypes
import numpy as np
from jax import lax
from jax.experimental import pallas as pl
from jax.experimental.pallas import tpu as pltpu
from jax.sharding import PartitionSpec as P

C = 16
MX = 48
MY = 48
MZ = 32
NX = 256
NY = 192
NZ = 512
GX = 64
GY = 8
XL = NX // GX
YL = NY // GY
KZL = MZ // GY
ROWS = XL * YL
BF = jnp.bfloat16
F32 = jnp.float32
LANES = 128
OWNED = MX * MY // GX
GXS = ("chip", "core")
TRIPLES = np.arange(48).reshape(16, 3).T.reshape(48)
PAIRS = np.arange(48).reshape(24, 2).T.reshape(48)


def angle(a, b, n):
    return (2.0 * np.pi / n) * ((np.asarray(a)[:, None] * np.asarray(b)[None, :]) % n).astype(np.float64)


def split(table):
    table = np.asarray(table, np.float64)
    high = table.astype(ml_dtypes.bfloat16)
    low = (table - high.astype(np.float64)).astype(ml_dtypes.bfloat16)
    return high, low


def z_tables():
    a = angle(np.arange(NZ), np.arange(MZ), NZ).astype(np.float32)
    tab = np.stack([np.cos(a), -np.sin(a)], 0).astype(ml_dtypes.bfloat16)
    tab = tab.reshape(2, NZ, GY, KZL)
    mid = np.zeros((2, NZ, KZL, 2, 2, GY), ml_dtypes.bfloat16)
    half = np.zeros((2, NZ, 2, 2, GY, KZL), ml_dtypes.bfloat16)
    inv = np.zeros((KZL, 2, 2, GY, 2, NZ), ml_dtypes.bfloat16)
    for h in range(2):
        mid[h, :, :, :, h] = np.transpose(tab, (1, 3, 0, 2))
        half[h, :, h] = np.transpose(tab, (1, 0, 2, 3))
        inv[:, :, h, :, h, :] = np.transpose(tab, (3, 0, 2, 1))
    return mid.reshape(2 * NZ, LANES), half.reshape(2 * NZ, LANES), inv.reshape(LANES, 2 * NZ)


def y_forward_table(kys):
    a = angle(kys, np.arange(NY), NY)
    return np.concatenate(split(np.cos(a) / math.sqrt(NY)) + split(np.sin(a) / math.sqrt(NY)), 0)


def x_forward_table():
    xs = np.arange(NX).reshape(GX, XL).T.reshape(NX)
    a = angle(TRIPLES, xs, NX)
    return np.concatenate(split(np.cos(a) / math.sqrt(NX)) + split(np.sin(a) / math.sqrt(NX)), 0)


def x_inverse_table():
    a = angle(np.arange(NX), TRIPLES, NX)
    return np.concatenate(split(np.cos(a)) + split(np.sin(a)), 1)


def y_inverse_table():
    a = angle(np.arange(NY), TRIPLES, NY)
    factor = 1.0 / math.sqrt(MX * MY * MZ)
    return np.concatenate(split(np.cos(a) * factor) + split(np.sin(a) * factor), 1)


def partial_tables():
    shift = (4 * np.arange(2)[:, None] + np.arange(2)[None, :]).reshape(4)
    lanes = 2 * (np.arange(LANES) // 64)
    a = (2.0 * np.pi / NX) * np.arange(MX)[:, None, None] * (shift[:, None] + lanes[None, :])[None]
    cos, sin = np.cos(a) / math.sqrt(NX), np.sin(a) / math.sqrt(NX)
    near = np.concatenate([cos, sin], 1).reshape(8 * MX, LANES)
    turn = np.concatenate([-sin, cos], 1).reshape(8 * MX, LANES)
    whole = 2.0 * np.pi / NX * np.arange(NX)
    whole = np.concatenate([np.cos(whole), np.sin(whole)])
    return [t.astype(np.float32) for t in (near, turn, whole)]


def expand_table():
    e = np.zeros((4, 2, 2, 8, 3, 2, 2, 8, C), ml_dtypes.bfloat16)
    for i in range(3):
        for r in range(2):
            for h in range(2):
                for c in range(8):
                    e[i, r, h, c, i, h, r, c, :] = 1.0
    return e.reshape(LANES, 6 * 2 * LANES)


def reorder_table():
    t = np.zeros((KZL, 2, C, 2, C, KZL), ml_dtypes.bfloat16)
    for k in range(KZL):
        for r in range(2):
            for c in range(C):
                t[k, r, c, r, c, k] = 1.0
    return t.reshape(LANES, LANES)


def dot(a, b):
    return jnp.dot(a, b, preferred_element_type=F32)


def dot_t(a, b):
    return lax.dot_general(a, b, (((1,), (1,)), ((), ())), preferred_element_type=F32)


def lane_of(shape):
    return lax.broadcasted_iota(jnp.int32, shape, len(shape) - 1)


def exchange(arrays, first):
    arrays = list(arrays)
    lane = lane_of(arrays[0].shape)
    bit = 1
    while bit < len(arrays):
        stride = first * bit
        clear = (lane & stride) == 0
        for i in range(len(arrays)):
            if i & bit:
                continue
            lo, hi = arrays[i], arrays[i | bit]
            arrays[i] = jnp.where(clear, lo, pltpu.roll(hi, stride, 1))
            arrays[i | bit] = jnp.where(clear, pltpu.roll(lo, LANES - stride, 1), hi)
        bit *= 2
    return arrays


def partner(v, stride):
    real = (lane_of(v.shape) & stride) == 0
    if stride == 64:
        return pltpu.roll(v, 64, 1), real
    return jnp.where(real, pltpu.roll(v, LANES - stride, 1), pltpu.roll(v, stride, 1)), real


def times_minus_i(v, stride):
    other, real = partner(v, stride)
    return jnp.where(real, other, -other)


def times_plus_i(v, stride):
    other, real = partner(v, stride)
    return jnp.where(real, -other, other)


def z_modes(even, odd, w_ref):
    modes = dot(even, w_ref[0:NZ, :]) + dot(odd, w_ref[NZ : 2 * NZ, :])
    modes = modes * (1.0 / math.sqrt(NZ))
    return [modes[i : i + ROWS] for i in range(0, modes.shape[0], ROWS)]


def k1(field_ref, w_ref, out_ref, x_ref, t_ref, sems):
    table = pltpu.make_async_copy(w_ref, t_ref, sems.at[8])
    table.start()
    copies = []
    for n in range(4):
        for h in range(2):
            part = pl.ds(8 * h + 2 * n, 2)
            copies.append(pltpu.make_async_copy(field_ref.at[part], x_ref.at[part], sems.at[2 * n + h]))
            copies[-1].start()
    table.wait()
    modes = []
    for n in range(4):
        copies[2 * n].wait()
        copies[2 * n + 1].wait()
        even = x_ref[2 * n : 2 * n + 2].reshape(2 * ROWS, NZ)
        odd = x_ref[8 + 2 * n : 10 + 2 * n].reshape(2 * ROWS, NZ)
        modes += z_modes(even, odd, t_ref)
    for p, v in enumerate(exchange(modes, 1)):
        out_ref[p] = v.astype(BF)


def y_transform(full, ty_ref, stride):
    out = []
    for x in range(full.shape[1] // YL):
        rows = jnp.concatenate([full[p, YL * x : YL * x + YL, :] for p in range(GY)], 0).astype(BF)
        t = dot(ty_ref[...], rows)
        cos, sin = t[0:48] + t[48:96], t[96:144] + t[144:192]
        out.append(cos + times_minus_i(sin, stride))
    return out


def ky_of(value, quarter):
    t = value + OWNED * quarter
    return t - jnp.where(t >= 48, 48, 0) - jnp.where(t >= 96, 48, 0)


def place():
    return 2 * lax.axis_index("chip") + lax.axis_index("core")


def k2(in_ref, spec_ref, ty_ref, out_ref, scratch):
    quarter = place() % 4
    row = lax.broadcasted_iota(jnp.int32, (MY, OWNED), 0)
    mode = ky_of(lax.broadcasted_iota(jnp.int32, (MY, OWNED), 1), quarter)
    select = (mode == 3 * (row % 16) + row // 16).astype(BF)
    for k in range(4):
        for b in range(KZL):
            block = spec_ref[pl.ds(512 * k + b, LANES, stride=KZL), :].astype(BF)
            moved = dot_t(select, block)
            for i in range(3):
                scratch[pl.ds(16 * b + 4 + 4 * i + k, 16, stride=64), :] = moved[16 * i : 16 * i + 16]
    for x, v in enumerate(y_transform(in_ref[...].astype(F32), ty_ref, 16)):
        parts = [v[0:16], v[16:32], v[32:48], jnp.zeros((16, LANES), F32)]
        for b, part in enumerate(exchange(parts, 32)):
            scratch[pl.ds(16 * b + x, 16, stride=64), :] = part
    out_ref[...] = scratch[...].astype(BF)


def k3(in_ref, tx_ref, e_ref, tinv_ref, out_ref, scratch):
    a = place() // 4
    scratch[...] = in_ref[...].astype(F32)
    data = jnp.concatenate([scratch[pl.ds(x, GX, stride=16), :] for x in range(XL)], 0).astype(BF)
    t = dot(tx_ref[...], data)
    fwd = t[0:48] + t[48:96] + times_minus_i(t[96:144] + t[144:192], 16)
    high = fwd.astype(BF)
    low = (fwd - high.astype(F32)).astype(BF)
    both = jnp.concatenate([high, low], 0)
    source = (
        jnp.where(a >= 12, 1, 0),
        1 + jnp.where(a >= 8, 1, 0),
        2 + jnp.where(a >= 4, 1, 0),
    )

    def weights(i, k):
        at = 4 + 4 * i + k
        return jnp.concatenate(
            [scratch[pl.ds(16 * source[r] + at, 16, stride=64), :] for r in range(3)], 0
        )

    group = lane_of((MX, LANES)) // 16
    mixed = jnp.zeros((MX, LANES), F32)
    for i in range(3):
        sums = [0.0, 0.0]
        for h in range(2):
            at = 256 * (2 * i + h)
            wide = dot(both, e_ref[:, at : at + 256])
            wide = wide[0:48] + wide[48:96]
            fr, fi = wide[:, 0:128], wide[:, 128:256]
            wr, wi = weights(i, h), weights(i, 2 + h)
            sums[0] += wr * fr - wi * fi
            sums[1] += wr * fi + wi * fr
        for r in range(2):
            v = sums[r]
            for stride in (64, 32, 16):
                v = v + pltpu.roll(v, stride, 1)
            mixed = jnp.where(group == 2 * i + r, v, mixed)
    mixed = mixed.astype(BF)
    turned = times_plus_i(mixed.astype(F32), 16).astype(BF)
    moved = [
        jnp.where(group >= 6, pltpu.roll(high.astype(F32), 96 - 32 * i, 1), 0.0)
        for i in range(3)
    ]
    moved = jnp.concatenate(moved, 0).astype(BF)
    row = lax.broadcasted_iota(jnp.int32, (NX, 3 * MX), 0)
    col = lax.broadcasted_iota(jnp.int32, (NX, 3 * MX), 1)
    owner = row // 4
    quarter = owner % 4
    back_one = jnp.where(quarter == 1, jnp.where(a >= 12, 1, 0), 0)
    back_one += jnp.where(quarter == 2, jnp.where(a >= 8, 1, 0), 0)
    r = jnp.minimum(quarter, 2) - back_one
    wanted = MX * (row % 4) + 16 * r + owner // 4
    select = (col == wanted).astype(BF)
    result = dot(tinv_ref[...], jnp.concatenate([mixed, mixed, turned, turned], 0))
    result += dot(select, moved)
    out_ref[...] = result.astype(BF)


def k4(in_ref, ty_ref, out_ref, fwd_ref, scratch):
    scratch[...] = in_ref[...].astype(F32)
    for x in range(XL):
        parts = [scratch[pl.ds(4 * b + x, 16, stride=16), :] for b in range(KZL)]
        parts = exchange(parts, 32)
        if x < 3:
            fwd_ref[16 * x : 16 * x + 16, :] = parts[3]
        v = jnp.concatenate(parts[0:3], 0)
        b = v.astype(BF)
        s = times_plus_i(v, 16).astype(BF)
        w = dot(ty_ref[...], jnp.concatenate([b, b, s, s], 0))
        for p in range(GY):
            out_ref[p, YL * x : YL * x + YL, :] = w[YL * p : YL * p + YL].astype(BF)


def slope(pre):
    square = pre * pre
    t = jnp.tanh(pre * (0.7978845608 + 0.7978845608 * 0.044715 * square))
    ramp = pre * (0.5 * 0.7978845608 + 1.5 * 0.7978845608 * 0.044715 * square)
    return (0.5 + 0.5 * t) + (1.0 - t * t) * ramp


def k5(waves_ref, field_ref, cot_ref, pw_ref, w_ref, zt_ref, out_ref, kron, grad):
    group = lax.broadcasted_iota(jnp.int32, (256, C), 0) // 16
    member = lax.broadcasted_iota(jnp.int32, (256, C), 1)
    one_hot = (group == member).astype(BF)
    wide = dot_t(dot_t(one_hot, pw_ref[...]).astype(BF), one_hot)
    r = lax.broadcasted_iota(jnp.int32, (256, 256), 0) % 16
    s = lax.broadcasted_iota(jnp.int32, (256, 256), 1) % 16
    kron[...] = jnp.where(r == s, wide, 0.0).astype(BF)
    for n in range(ROWS // 16):
        rows = slice(16 * n, 16 * n + 16)
        parts = exchange([waves_ref[p, rows, :].astype(F32) for p in range(GY)], 1)
        waves = jnp.concatenate(parts, 0).astype(BF)
        x = field_ref[:, rows, :].reshape(C * 16, NZ)
        for h in range(2):
            pre = dot(waves, zt_ref[:, NZ * h : NZ * h + NZ])
            pre += dot(kron[128 * h : 128 * h + 128, :], x)
            cot = cot_ref[8 * h : 8 * h + 8, rows, :].reshape(128, NZ).astype(F32)
            grad[8 * h : 8 * h + 8, rows, :] = (cot * slope(pre)).astype(BF).reshape(8, 16, NZ)
    even = grad[0:8].reshape(8 * ROWS, NZ)
    odd = grad[8:16].reshape(8 * ROWS, NZ)
    for p, v in enumerate(exchange(z_modes(even, odd, w_ref), 4)):
        for core, part in enumerate(exchange([v[0:48], v[48:96]], 64)):
            out_ref[8 * core + p] = part.astype(BF)


def k6(in_ref, ty_ref, near_ref, turn_ref, cs_ref, out_ref, factors):
    chip = lax.axis_index("chip")
    for kx in range(MX):
        at = (8 * kx * chip) & (NX - 1)
        rows = slice(8 * kx, 8 * kx + 8)
        factors[rows, :] = near_ref[rows, :] * cs_ref[at] + turn_ref[rows, :] * cs_ref[NX + at]
    full = in_ref[...].astype(F32)
    values = []
    for core in range(2):
        values += y_transform(full[8 * core : 8 * core + 8], ty_ref, 32)
    turned = [times_minus_i(v, 32) for v in values]
    low = lane_of((24, LANES)) < 64

    terms = values + turned
    for kx in range(0, MX, 2):
        rows = []
        for at in (8 * kx, 8 * kx + 8):
            acc = terms[0] * factors[at : at + 1, :]
            for n in range(1, 8):
                acc += terms[n] * factors[at + n : at + n + 1, :]
            even, odd = acc[0:24], acc[24:48]
            rows.append(jnp.where(low, even, odd) + pltpu.roll(jnp.where(low, odd, even), 64, 1))
        out_ref[24 * kx : 24 * kx + 48, :] = jnp.concatenate(rows, 0).astype(BF)


def k7(in_ref, fwd_ref, reorder_ref, spec_ref, mom_ref, out_ref, scratch):
    quarter = place() % 4
    total = in_ref[0:72, :].astype(F32)
    for g in range(1, 16):
        total += in_ref[72 * g : 72 * g + 72, :].astype(F32)
    scratch[0:72, :] = total
    scratch[72:80, :] = jnp.zeros((8, LANES), F32)
    total = scratch[0:40, :] + scratch[36:76, :]
    row = lax.broadcasted_iota(jnp.int32, (2 * LANES, 40), 0)
    col = lax.broadcasted_iota(jnp.int32, (2 * LANES, 40), 1)
    mode = row % LANES
    select = ((col == 18 * (row // LANES) + mode // 2) & (mode < OWNED)).astype(F32)
    moved = jnp.dot(select, total, precision=lax.Precision.HIGHEST, preferred_element_type=F32)
    first, second = moved[0:LANES], moved[LANES : 2 * LANES]
    odd = lax.broadcasted_iota(jnp.int32, (LANES, LANES), 0) % 2
    upper = lane_of((LANES, LANES)) // 64
    grads = jnp.where(upper == 0, first, second)
    other = jnp.where(upper == 0, pltpu.roll(first, 64, 1), pltpu.roll(second, 64, 1))
    grads = jnp.where(upper == odd, grads, other)
    row = lax.broadcasted_iota(jnp.int32, (LANES, MY), 0)
    col = lax.broadcasted_iota(jnp.int32, (LANES, MY), 1)
    hit = (ky_of(row, quarter) == 3 * (col % 16) + col // 16) & (row < OWNED)
    fwd = dot(hit.astype(BF), fwd_ref[...].astype(BF)).astype(BF)
    fwd = dot(fwd, reorder_ref[...])
    grads = grads.T[:, 0:OWNED]
    fwd = fwd.T[:, 0:OWNED]
    grad_r = jnp.concatenate([grads[0:32], grads[64:96]], 0)
    grad_i = jnp.concatenate([grads[32:64], grads[96:128]], 0)
    for c in range(C):
        fr = fwd[4 * c : 4 * c + 4]
        fi = fwd[64 + 4 * c : 68 + 4 * c]
        fr = jnp.concatenate([fr] * 16, 0)
        fi = jnp.concatenate([fi] * 16, 0)
        d_real = grad_r * fr + grad_i * fi
        d_imag = grad_i * fr - grad_r * fi
        out_ref[0, c] = mom_ref[0, c] - 0.25 * (d_real + 2.0 * C * spec_ref[0, c])
        out_ref[1, c] = mom_ref[1, c] - 0.25 * (d_imag + 2.0 * C * spec_ref[1, c])


def call(body, out, *args, scratch=(), smem=(), hbm=()):
    specs = [
        pl.BlockSpec(memory_space=pltpu.SMEM if i in smem else pltpu.HBM if i in hbm else pltpu.VMEM)
        for i in range(len(args))
    ]
    vmem = pl.BlockSpec(memory_space=pltpu.VMEM)
    return pl.pallas_call(
        body,
        out_shape=out,
        in_specs=specs,
        out_specs=jax.tree.map(lambda _: vmem, out),
        scratch_shapes=list(scratch),
        compiler_params=pltpu.CompilerParams(vmem_limit_bytes=40 * 1024 * 1024),
    )(*args)


def swap(value, axis):
    return lax.all_to_all(value, axis, split_axis=0, concat_axis=0, tiled=True)


def on_device(field, pointwise, spectral, momentum, cotangent):
    field = field.reshape(C, ROWS, NZ)
    cotangent = cotangent.reshape(C, ROWS, NZ)
    spectral = jnp.transpose(spectral, (1, 2, 3, 4, 0))
    momentum = jnp.transpose(momentum, (1, 2, 3, 4, 0))
    z_mid, z_half, z_inv = [jnp.asarray(t) for t in z_tables()]
    zshape = jax.ShapeDtypeStruct((GY, ROWS, LANES), BF)

    zmodes = call(
        k1,
        zshape,
        pltpu.with_memory_space_constraint(field, pltpu.HBM),
        pltpu.with_memory_space_constraint(z_mid, pltpu.HBM),
        hbm=(0, 1),
        scratch=[
            pltpu.VMEM((C, ROWS, NZ), BF),
            pltpu.VMEM((2 * NZ, LANES), BF),
            pltpu.SemaphoreType.DMA((9,)),
        ],
    )
    zmodes = swap(zmodes, "gy")
    sent = call(
        k2,
        jax.ShapeDtypeStruct((GX * 16, LANES), BF),
        zmodes,
        spectral.reshape(2 * C * C * KZL, OWNED),
        jnp.asarray(y_forward_table(TRIPLES)),
        scratch=[pltpu.VMEM((GX * 16, LANES), F32)],
    )
    got = swap(sent.reshape(GX, 16, LANES), GXS).reshape(GX * 16, LANES)
    sent = call(
        k3,
        jax.ShapeDtypeStruct((NX, LANES), BF),
        got,
        jnp.asarray(x_forward_table()),
        jnp.asarray(expand_table()),
        jnp.asarray(x_inverse_table()),
        scratch=[pltpu.VMEM((GX * 16, LANES), F32)],
    )
    back = swap(sent.reshape(GX, XL, LANES), GXS).reshape(NX, LANES)
    waves, fwd = call(
        k4,
        (zshape, jax.ShapeDtypeStruct((MY, LANES), F32)),
        back,
        jnp.asarray(y_inverse_table()),
        scratch=[pltpu.VMEM((NX, LANES), F32)],
    )
    zgrads = call(
        k5,
        jax.ShapeDtypeStruct((2 * GY, ROWS // 2, LANES), BF),
        swap(waves, "gy"),
        field,
        cotangent,
        pointwise,
        z_half,
        z_inv,
        scratch=[pltpu.VMEM((256, 256), BF), pltpu.VMEM((C, ROWS, NZ), BF)],
    )
    partial = call(
        k6,
        jax.ShapeDtypeStruct((MX * MY // 2, LANES), BF),
        swap(zgrads, ("core", "gy")),
        jnp.asarray(y_forward_table(PAIRS)),
        *[jnp.asarray(t) for t in partial_tables()],
        smem=(4,),
        scratch=[pltpu.VMEM((8 * MX, LANES), F32)],
    )
    partial = swap(partial.reshape(GX, OWNED // 4, 2, LANES), GXS).reshape(MX * MY // 2, LANES)
    result = call(
        k7,
        jax.ShapeDtypeStruct((2, C, C * KZL, OWNED), F32),
        partial,
        fwd,
        jnp.asarray(reorder_table()),
        spectral.reshape(2, C, C * KZL, OWNED),
        momentum.reshape(2, C, C * KZL, OWNED),
        scratch=[pltpu.VMEM((80, LANES), F32)],
    )
    result = result.reshape(2, C, C, KZL, OWNED)
    return jnp.transpose(result, (4, 0, 1, 2, 3))


def solution(mesh):
    chips = jax.sharding.Mesh(mesh.devices.reshape(GX // 2, 2, GY), ("chip", "core", "gy"))
    in_specs = (
        P(None, GXS, "gy", None),
        P(),
        P(GXS, None, None, None, "gy"),
        P(GXS, None, None, None, "gy"),
        P(None, GXS, "gy", None),
    )
    out_specs = P(GXS, None, None, None, "gy")
    return jax.shard_map(
        on_device, mesh=chips, in_specs=in_specs, out_specs=out_specs, check_vma=False
    )
```

```python
import math

import jax
import jax.numpy as jnp
import ml_dtypes
import numpy as np
from jax import lax
from jax.experimental import pallas as pl
from jax.experimental.pallas import tpu as pltpu
from jax.sharding import PartitionSpec as P

C = 16
MX = 48
MY = 48
MZ = 32
NX = 256
NY = 192
NZ = 512
GX = 64
GY = 8
XL = NX // GX
YL = NY // GY
KZL = MZ // GY
ROWS = XL * YL
BF = jnp.bfloat16
F32 = jnp.float32
LANES = 128
OWNED = MX * MY // GX
GXS = ("chip", "core")
TRIPLES = np.arange(48).reshape(16, 3).T.reshape(48)
PAIRS = np.arange(48).reshape(24, 2).T.reshape(48)


def angle(a, b, n):
    return (2.0 * np.pi / n) * ((np.asarray(a)[:, None] * np.asarray(b)[None, :]) % n).astype(np.float64)


def split(table):
    table = np.asarray(table, np.float64)
    high = table.astype(ml_dtypes.bfloat16)
    low = (table - high.astype(np.float64)).astype(ml_dtypes.bfloat16)
    return high, low


def z_tables():
    a = angle(np.arange(NZ), np.arange(MZ), NZ).astype(np.float32)
    tab = np.stack([np.cos(a), -np.sin(a)], 0).astype(ml_dtypes.bfloat16)
    tab = tab.reshape(2, NZ, GY, KZL)
    mid = np.zeros((2, NZ, KZL, 2, 2, GY), ml_dtypes.bfloat16)
    half = np.zeros((2, NZ, 2, 2, GY, KZL), ml_dtypes.bfloat16)
    inv = np.zeros((KZL, 2, 2, GY, 2, NZ), ml_dtypes.bfloat16)
    for h in range(2):
        mid[h, :, :, :, h] = np.transpose(tab, (1, 3, 0, 2))
        half[h, :, h] = np.transpose(tab, (1, 0, 2, 3))
        inv[:, :, h, :, h, :] = np.transpose(tab, (3, 0, 2, 1))
    return mid.reshape(2 * NZ, LANES), half.reshape(2 * NZ, LANES), inv.reshape(LANES, 2 * NZ)


def y_forward_table(kys):
    a = angle(kys, np.arange(NY), NY)
    return np.concatenate(split(np.cos(a) / math.sqrt(NY)) + split(np.sin(a) / math.sqrt(NY)), 0)


def x_forward_table():
    xs = np.arange(NX).reshape(GX, XL).T.reshape(NX)
    a = angle(TRIPLES, xs, NX)
    return np.concatenate(split(np.cos(a) / math.sqrt(NX)) + split(np.sin(a) / math.sqrt(NX)), 0)


def x_inverse_table():
    a = angle(np.arange(NX), TRIPLES, NX)
    return np.concatenate(split(np.cos(a)) + split(np.sin(a)), 1)


def y_inverse_table():
    a = angle(np.arange(NY), TRIPLES, NY)
    factor = 1.0 / math.sqrt(MX * MY * MZ)
    return np.concatenate(split(np.cos(a) * factor) + split(np.sin(a) * factor), 1)


def partial_tables():
    shift = (4 * np.arange(2)[:, None] + np.arange(2)[None, :]).reshape(4)
    lanes = 2 * (np.arange(LANES) // 64)
    a = (2.0 * np.pi / NX) * np.arange(MX)[:, None, None] * (shift[:, None] + lanes[None, :])[None]
    cos, sin = np.cos(a) / math.sqrt(NX), np.sin(a) / math.sqrt(NX)
    near = np.concatenate([cos, sin], 1).reshape(8 * MX, LANES)
    turn = np.concatenate([-sin, cos], 1).reshape(8 * MX, LANES)
    eighth = 2.0 * np.pi / 32 * np.arange(32)
    chip = np.repeat(np.stack([np.cos(eighth), np.sin(eighth)], 1), LANES, 1)
    parts = []
    for _ in range(3):
        parts.append(chip.astype(ml_dtypes.bfloat16))
        chip = chip - parts[-1].astype(np.float64)
    return near.astype(np.float32), turn.astype(np.float32), np.concatenate(parts, 0)


def expand_table():
    e = np.zeros((4, 2, 2, 8, 3, 2, 2, 8, C), ml_dtypes.bfloat16)
    for i in range(3):
        for r in range(2):
            for h in range(2):
                for c in range(8):
                    e[i, r, h, c, i, h, r, c, :] = 1.0
    return e.reshape(LANES, 6 * 2 * LANES)


def reorder_table():
    t = np.zeros((KZL, 2, C, 2, C, KZL), ml_dtypes.bfloat16)
    for k in range(KZL):
        for r in range(2):
            for c in range(C):
                t[k, r, c, r, c, k] = 1.0
    return t.reshape(LANES, LANES)


def dot(a, b):
    return jnp.dot(a, b, preferred_element_type=F32)


def dot_t(a, b):
    return lax.dot_general(a, b, (((1,), (1,)), ((), ())), preferred_element_type=F32)


def lane_of(shape):
    return lax.broadcasted_iota(jnp.int32, shape, len(shape) - 1)


def exchange(arrays, first):
    arrays = list(arrays)
    lane = lane_of(arrays[0].shape)
    bit = 1
    while bit < len(arrays):
        stride = first * bit
        clear = (lane & stride) == 0
        for i in range(len(arrays)):
            if i & bit:
                continue
            lo, hi = arrays[i], arrays[i | bit]
            arrays[i] = jnp.where(clear, lo, pltpu.roll(hi, stride, 1))
            arrays[i | bit] = jnp.where(clear, pltpu.roll(lo, LANES - stride, 1), hi)
        bit *= 2
    return arrays


def partner(v, stride):
    real = (lane_of(v.shape) & stride) == 0
    if stride == 64:
        return pltpu.roll(v, 64, 1), real
    return jnp.where(real, pltpu.roll(v, LANES - stride, 1), pltpu.roll(v, stride, 1)), real


def times_minus_i(v, stride):
    other, real = partner(v, stride)
    return jnp.where(real, other, -other)


def times_plus_i(v, stride):
    other, real = partner(v, stride)
    return jnp.where(real, -other, other)


def z_modes(even, odd, w_ref):
    modes = dot(even, w_ref[0:NZ, :]) + dot(odd, w_ref[NZ : 2 * NZ, :])
    modes = modes * (1.0 / math.sqrt(NZ))
    return [modes[i : i + ROWS] for i in range(0, modes.shape[0], ROWS)]


def expand_pointwise(pw):
    group = lax.broadcasted_iota(jnp.int32, (256, C), 0) // 16
    member = lax.broadcasted_iota(jnp.int32, (256, C), 1)
    one_hot = (group == member).astype(BF)
    wide = dot_t(dot_t(one_hot, pw).astype(BF), one_hot)
    r = lax.broadcasted_iota(jnp.int32, (256, 256), 0) % 16
    s = lax.broadcasted_iota(jnp.int32, (256, 256), 1) % 16
    return jnp.where(r == s, wide, 0.0).astype(BF)


def k1(field_ref, w_ref, pw_ref, out_ref, kron_ref, x_ref, t_ref, p_ref, sems):
    small = pltpu.make_async_copy(pw_ref, p_ref, sems.at[9])
    small.start()
    table = pltpu.make_async_copy(w_ref, t_ref, sems.at[8])
    table.start()
    copies = []
    for n in range(4):
        for h in range(2):
            part = pl.ds(8 * h + 2 * n, 2)
            copies.append(pltpu.make_async_copy(field_ref.at[part], x_ref.at[part], sems.at[2 * n + h]))
            copies[-1].start()
    small.wait()
    kron_ref[...] = expand_pointwise(p_ref[...])
    table.wait()
    modes = []
    for n in range(4):
        copies[2 * n].wait()
        copies[2 * n + 1].wait()
        even = x_ref[2 * n : 2 * n + 2].reshape(2 * ROWS, NZ)
        odd = x_ref[8 + 2 * n : 10 + 2 * n].reshape(2 * ROWS, NZ)
        modes += z_modes(even, odd, t_ref)
    for p, v in enumerate(exchange(modes, 1)):
        out_ref[p] = v.astype(BF)


def y_transform(full, ty_ref, stride):
    out = []
    for x in range(full.shape[1] // YL):
        rows = jnp.concatenate([full[p, YL * x : YL * x + YL, :] for p in range(GY)], 0).astype(BF)
        t = dot(ty_ref[...], rows)
        cos, sin = t[0:48] + t[48:96], t[96:144] + t[144:192]
        out.append(cos + times_minus_i(sin, stride))
    return out


def ky_of(value, quarter):
    t = value + OWNED * quarter
    return t - jnp.where(t >= 48, 48, 0) - jnp.where(t >= 96, 48, 0)


def place():
    return 2 * lax.axis_index("chip") + lax.axis_index("core")


def k2(in_ref, spec_ref, ty_ref, out_ref, scratch):
    quarter = place() % 4
    row = lax.broadcasted_iota(jnp.int32, (MY, OWNED), 0)
    mode = ky_of(lax.broadcasted_iota(jnp.int32, (MY, OWNED), 1), quarter)
    select = (mode == 3 * (row % 16) + row // 16).astype(BF)
    for k in range(4):
        for b in range(KZL):
            block = spec_ref[pl.ds(512 * k + b, LANES, stride=KZL), :].astype(BF)
            moved = dot_t(select, block)
            for i in range(3):
                scratch[pl.ds(16 * b + 4 + 4 * i + k, 16, stride=64), :] = moved[16 * i : 16 * i + 16]
    for x, v in enumerate(y_transform(in_ref[...].astype(F32), ty_ref, 16)):
        parts = [v[0:16], v[16:32], v[32:48], jnp.zeros((16, LANES), F32)]
        for b, part in enumerate(exchange(parts, 32)):
            scratch[pl.ds(16 * b + x, 16, stride=64), :] = part
    out_ref[...] = scratch[...].astype(BF)


def fold(arrays):
    lane = lane_of(arrays[0].shape)
    zero = jnp.zeros_like(arrays[0])
    arrays = arrays + [zero, zero]
    for stride in (64, 32, 16):
        n = len(arrays) // 2
        clear = (lane & stride) == 0
        merged = []
        for lo, hi in zip(arrays[:n], arrays[n:]):
            moved = jnp.where(clear, hi, lo)
            back = pltpu.roll(moved, stride, 1)
            if stride < 64:
                back = jnp.where(clear, pltpu.roll(moved, LANES - stride, 1), back)
            merged.append(jnp.where(clear, lo, hi) + back)
        arrays = merged
    return arrays[0]


def k3(in_ref, tx_ref, e_ref, tinv_ref, out_ref, scratch):
    a = place() // 4
    scratch[...] = in_ref[...].astype(F32)
    data = jnp.concatenate([scratch[pl.ds(x, GX, stride=16), :] for x in range(XL)], 0).astype(BF)
    t = dot(tx_ref[...], data)
    fwd = t[0:48] + t[48:96] + times_minus_i(t[96:144] + t[144:192], 16)
    fwd = fwd.astype(BF)
    source = (
        jnp.where(a >= 12, 1, 0),
        1 + jnp.where(a >= 8, 1, 0),
        2 + jnp.where(a >= 4, 1, 0),
    )

    def weights(i, k):
        at = 4 + 4 * i + k
        return jnp.concatenate(
            [scratch[pl.ds(16 * source[r] + at, 16, stride=64), :] for r in range(3)], 0
        )

    sums = []
    for i in range(3):
        real, imag = 0.0, 0.0
        for h in range(2):
            at = 256 * (2 * i + h)
            wide = dot(fwd, e_ref[:, at : at + 256])
            fr, fi = wide[:, 0:128], wide[:, 128:256]
            wr, wi = weights(i, h), weights(i, 2 + h)
            real += wr * fr - wi * fi
            imag += wr * fi + wi * fr
        sums += [real, imag]
    mixed = fold(sums)
    mixed = mixed.astype(BF)
    turned = times_plus_i(mixed.astype(F32), 16).astype(BF)
    moved = [
        jnp.where(lane_of(fwd.shape) >= 96, pltpu.roll(fwd.astype(F32), 96 - 32 * i, 1), 0.0)
        for i in range(3)
    ]
    moved = jnp.concatenate(moved, 0).astype(BF)
    row = lax.broadcasted_iota(jnp.int32, (NX, 3 * MX), 0)
    col = lax.broadcasted_iota(jnp.int32, (NX, 3 * MX), 1)
    owner = row // 4
    quarter = owner % 4
    back_one = jnp.where(quarter == 1, jnp.where(a >= 12, 1, 0), 0)
    back_one += jnp.where(quarter == 2, jnp.where(a >= 8, 1, 0), 0)
    r = jnp.minimum(quarter, 2) - back_one
    wanted = MX * (row % 4) + 16 * r + owner // 4
    select = (col == wanted).astype(BF)
    result = dot(tinv_ref[...], jnp.concatenate([mixed, mixed, turned, turned], 0))
    result += dot(select, moved)
    out_ref[...] = result.astype(BF)


def k4(in_ref, ty_ref, out_ref, fwd_ref, scratch):
    scratch[...] = in_ref[...].astype(F32)
    for x in range(XL):
        parts = [scratch[pl.ds(4 * b + x, 16, stride=16), :] for b in range(KZL)]
        parts = exchange(parts, 32)
        if x < 3:
            fwd_ref[16 * x : 16 * x + 16, :] = parts[3]
        v = jnp.concatenate(parts[0:3], 0)
        b = v.astype(BF)
        s = times_plus_i(v, 16).astype(BF)
        w = dot(ty_ref[...], jnp.concatenate([b, b, s, s], 0))
        for p in range(GY):
            out_ref[p, YL * x : YL * x + YL, :] = w[YL * p : YL * p + YL].astype(BF)


def slope(pre):
    square = pre * pre
    t = jnp.tanh(pre * (0.7978845608 + 0.7978845608 * 0.044715 * square))
    ramp = pre * (0.5 * 0.7978845608 + 1.5 * 0.7978845608 * 0.044715 * square)
    return (0.5 + 0.5 * t) + (1.0 - t * t) * ramp


def k5(waves_ref, field_ref, cot_ref, kron, w_ref, zt_ref, out_ref, grad):
    for n in range(ROWS // 16):
        rows = slice(16 * n, 16 * n + 16)
        parts = exchange([waves_ref[p, rows, :].astype(F32) for p in range(GY)], 1)
        waves = jnp.concatenate(parts, 0).astype(BF)
        x = field_ref[:, rows, :].reshape(C * 16, NZ)
        mapped = dot(kron[...], x)
        for h in range(2):
            pre = dot(waves, zt_ref[:, NZ * h : NZ * h + NZ]) + mapped[128 * h : 128 * h + 128]
            cot = cot_ref[8 * h : 8 * h + 8, rows, :].reshape(128, NZ).astype(F32)
            grad[8 * h : 8 * h + 8, rows, :] = (cot * slope(pre)).astype(BF).reshape(8, 16, NZ)
    even = grad[0:8].reshape(8 * ROWS, NZ)
    odd = grad[8:16].reshape(8 * ROWS, NZ)
    for p, v in enumerate(exchange(z_modes(even, odd, w_ref), 4)):
        for core, part in enumerate(exchange([v[0:48], v[48:96]], 64)):
            out_ref[8 * core + p] = part.astype(BF)


def k6(in_ref, ty_ref, near_ref, turn_ref, chip_ref, out_ref, factors):
    kx = lax.broadcasted_iota(jnp.int32, (MX, 96), 0)
    member = lax.broadcasted_iota(jnp.int32, (MX, 96), 1) % 32
    one_hot = (member == (kx * lax.axis_index("chip")) % 32).astype(BF)
    chip = dot(one_hot, chip_ref[...])
    for kx in range(MX):
        rows = slice(8 * kx, 8 * kx + 8)
        cos, sin = chip[kx : kx + 1, 0:128], chip[kx : kx + 1, 128:256]
        factors[rows, :] = near_ref[rows, :] * cos + turn_ref[rows, :] * sin
    full = in_ref[...].astype(F32)
    values = []
    for core in range(2):
        values += y_transform(full[8 * core : 8 * core + 8], ty_ref, 32)
    turned = [times_minus_i(v, 32) for v in values]
    low = lane_of((24, LANES)) < 64

    terms = values + turned
    for kx in range(0, MX, 2):
        rows = []
        for at in (8 * kx, 8 * kx + 8):
            acc = terms[0] * factors[at : at + 1, :]
            for n in range(1, 8):
                acc += terms[n] * factors[at + n : at + n + 1, :]
            even, odd = acc[0:24], acc[24:48]
            rows.append(jnp.where(low, even, odd) + pltpu.roll(jnp.where(low, odd, even), 64, 1))
        out_ref[24 * kx : 24 * kx + 48, :] = jnp.concatenate(rows, 0).astype(BF)


def k7(in_ref, fwd_ref, reorder_ref, spec_ref, mom_ref, out_ref, scratch, result, sems):
    quarter = place() % 4
    total = in_ref[0:72, :].astype(F32)
    for g in range(1, 16):
        total += in_ref[72 * g : 72 * g + 72, :].astype(F32)
    scratch[0:72, :] = total
    scratch[72:80, :] = jnp.zeros((8, LANES), F32)
    total = scratch[0:40, :] + scratch[36:76, :]
    row = lax.broadcasted_iota(jnp.int32, (2 * LANES, 120), 0)
    col = lax.broadcasted_iota(jnp.int32, (2 * LANES, 120), 1) % 40
    mode = row % LANES
    select = ((col == 18 * (row // LANES) + mode // 2) & (mode < OWNED)).astype(BF)
    parts = []
    for _ in range(3):
        parts.append(total.astype(BF).astype(F32))
        total = total - parts[-1]
    moved = dot(select, jnp.concatenate(parts, 0).astype(BF))
    first, second = moved[0:LANES], moved[LANES : 2 * LANES]
    odd = lax.broadcasted_iota(jnp.int32, (LANES, LANES), 0) % 2
    upper = lane_of((LANES, LANES)) // 64
    grads = jnp.where(upper == 0, first, second)
    other = jnp.where(upper == 0, pltpu.roll(first, 64, 1), pltpu.roll(second, 64, 1))
    grads = jnp.where(upper == odd, grads, other)
    row = lax.broadcasted_iota(jnp.int32, (LANES, MY), 0)
    col = lax.broadcasted_iota(jnp.int32, (LANES, MY), 1)
    hit = (ky_of(row, quarter) == 3 * (col % 16) + col // 16) & (row < OWNED)
    fwd = dot(hit.astype(BF), fwd_ref[...].astype(BF)).astype(BF)
    fwd = dot(fwd, reorder_ref[...])
    grads = grads.T[:, 0:OWNED]
    fwd = fwd.T[:, 0:OWNED]
    grad_r = jnp.concatenate([grads[0:32], grads[64:96]], 0)
    grad_i = jnp.concatenate([grads[32:64], grads[96:128]], 0)
    copies = []
    for c in range(C):
        fr = fwd[4 * c : 4 * c + 4]
        fi = fwd[64 + 4 * c : 68 + 4 * c]
        fr = jnp.concatenate([fr] * 16, 0)
        fi = jnp.concatenate([fi] * 16, 0)
        d_real = grad_r * fr + grad_i * fi
        d_imag = grad_i * fr - grad_r * fi
        result[0, c] = mom_ref[0, c] - 0.25 * (d_real + 2.0 * C * spec_ref[0, c])
        result[1, c] = mom_ref[1, c] - 0.25 * (d_imag + 2.0 * C * spec_ref[1, c])
        if c % 4 == 3:
            for r in range(2):
                part = pl.ds(c - 3, 4)
                copy = pltpu.make_async_copy(
                    result.at[r, part], out_ref.at[r, part], sems.at[2 * (c // 4) + r]
                )
                copy.start()
                copies.append(copy)
    for copy in copies:
        copy.wait()


def call(body, out, *args, scratch=(), hbm=(), out_space=pltpu.VMEM):
    specs = [
        pl.BlockSpec(memory_space=pltpu.HBM if i in hbm else pltpu.VMEM) for i in range(len(args))
    ]
    out_spec = pl.BlockSpec(memory_space=out_space)
    return pl.pallas_call(
        body,
        out_shape=out,
        in_specs=specs,
        out_specs=jax.tree.map(lambda _: out_spec, out),
        scratch_shapes=list(scratch),
        compiler_params=pltpu.CompilerParams(vmem_limit_bytes=40 * 1024 * 1024),
    )(*args)


def swap(value, axis):
    return lax.all_to_all(value, axis, split_axis=0, concat_axis=0, tiled=True)


def on_device(field, pointwise, spectral, momentum, cotangent):
    field = field.reshape(C, ROWS, NZ)
    cotangent = cotangent.reshape(C, ROWS, NZ)
    spectral = jnp.transpose(spectral, (1, 2, 3, 4, 0))
    momentum = jnp.transpose(momentum, (1, 2, 3, 4, 0))
    z_mid, z_half, z_inv = [jnp.asarray(t) for t in z_tables()]
    zshape = jax.ShapeDtypeStruct((GY, ROWS, LANES), BF)

    zmodes, kron = call(
        k1,
        (zshape, jax.ShapeDtypeStruct((256, 256), BF)),
        pltpu.with_memory_space_constraint(field, pltpu.HBM),
        pltpu.with_memory_space_constraint(z_mid, pltpu.HBM),
        pltpu.with_memory_space_constraint(pointwise, pltpu.HBM),
        hbm=(0, 1, 2),
        scratch=[
            pltpu.VMEM((C, ROWS, NZ), BF),
            pltpu.VMEM((2 * NZ, LANES), BF),
            pltpu.VMEM((C, C), BF),
            pltpu.SemaphoreType.DMA((10,)),
        ],
    )
    zmodes = swap(zmodes, "gy")
    sent = call(
        k2,
        jax.ShapeDtypeStruct((GX * 16, LANES), BF),
        zmodes,
        spectral.reshape(2 * C * C * KZL, OWNED),
        jnp.asarray(y_forward_table(TRIPLES)),
        scratch=[pltpu.VMEM((GX * 16, LANES), F32)],
    )
    got = swap(sent.reshape(GX, 16, LANES), GXS).reshape(GX * 16, LANES)
    sent = call(
        k3,
        jax.ShapeDtypeStruct((NX, LANES), BF),
        got,
        jnp.asarray(x_forward_table()),
        jnp.asarray(expand_table()),
        jnp.asarray(x_inverse_table()),
        scratch=[pltpu.VMEM((GX * 16, LANES), F32)],
    )
    back = swap(sent.reshape(GX, XL, LANES), GXS).reshape(NX, LANES)
    waves, fwd = call(
        k4,
        (zshape, jax.ShapeDtypeStruct((MY, LANES), F32)),
        back,
        jnp.asarray(y_inverse_table()),
        scratch=[pltpu.VMEM((NX, LANES), F32)],
    )
    zgrads = call(
        k5,
        jax.ShapeDtypeStruct((2 * GY, ROWS // 2, LANES), BF),
        swap(waves, "gy"),
        field,
        cotangent,
        kron,
        z_half,
        z_inv,
        scratch=[pltpu.VMEM((C, ROWS, NZ), BF)],
    )
    partial = call(
        k6,
        jax.ShapeDtypeStruct((MX * MY // 2, LANES), BF),
        swap(zgrads, ("core", "gy")),
        jnp.asarray(y_forward_table(PAIRS)),
        *[jnp.asarray(t) for t in partial_tables()],
        scratch=[pltpu.VMEM((8 * MX, LANES), F32)],
    )
    partial = swap(partial.reshape(GX, OWNED // 4, 2, LANES), GXS).reshape(MX * MY // 2, LANES)
    result = call(
        k7,
        jax.ShapeDtypeStruct((2, C, C * KZL, OWNED), F32),
        partial,
        fwd,
        jnp.asarray(reorder_table()),
        spectral.reshape(2, C, C * KZL, OWNED),
        momentum.reshape(2, C, C * KZL, OWNED),
        scratch=[
            pltpu.VMEM((80, LANES), F32),
            pltpu.VMEM((2, C, C * KZL, OWNED), F32),
            pltpu.SemaphoreType.DMA((8,)),
        ],
        out_space=pltpu.HBM,
    )
    result = result.reshape(2, C, C, KZL, OWNED)
    return jnp.transpose(result, (4, 0, 1, 2, 3))


def solution(mesh):
    chips = jax.sharding.Mesh(mesh.devices.reshape(GX // 2, 2, GY), ("chip", "core", "gy"))
    in_specs = (
        P(None, GXS, "gy", None),
        P(),
        P(GXS, None, None, None, "gy"),
        P(GXS, None, None, None, "gy"),
        P(None, GXS, "gy", None),
    )
    out_specs = P(GXS, None, None, None, "gy")
    return jax.shard_map(
        on_device, mesh=chips, in_specs=in_specs, out_specs=out_specs, check_vma=False
    )
```

```python
import math

import jax
import jax.numpy as jnp
import ml_dtypes
import numpy as np
from jax import lax
from jax.experimental import pallas as pl
from jax.experimental.pallas import tpu as pltpu
from jax.sharding import PartitionSpec as P

C = 16
MX = 48
MY = 48
MZ = 32
NX = 256
NY = 192
NZ = 512
GX = 64
GY = 8
XL = NX // GX
YL = NY // GY
KZL = MZ // GY
ROWS = XL * YL
BF = jnp.bfloat16
F32 = jnp.float32
LANES = 128
OWNED = MX * MY // GX
GXS = ("chip", "core")
TRIPLES = np.arange(48).reshape(16, 3).T.reshape(48)
PAIRS = np.arange(48).reshape(24, 2).T.reshape(48)


def angle(a, b, n):
    return (2.0 * np.pi / n) * ((np.asarray(a)[:, None] * np.asarray(b)[None, :]) % n).astype(np.float64)


def split(table):
    table = np.asarray(table, np.float64)
    high = table.astype(ml_dtypes.bfloat16)
    low = (table - high.astype(np.float64)).astype(ml_dtypes.bfloat16)
    return high, low


def z_tables():
    a = angle(np.arange(NZ), np.arange(MZ), NZ).astype(np.float32)
    tab = np.stack([np.cos(a), -np.sin(a)], 0).astype(ml_dtypes.bfloat16)
    tab = tab.reshape(2, NZ, GY, KZL)
    mid = np.zeros((2, NZ, KZL, 2, 2, GY), ml_dtypes.bfloat16)
    half = np.zeros((2, NZ, 2, 2, GY, KZL), ml_dtypes.bfloat16)
    inv = np.zeros((KZL, 2, 2, GY, 2, NZ), ml_dtypes.bfloat16)
    for h in range(2):
        mid[h, :, :, :, h] = np.transpose(tab, (1, 3, 0, 2))
        half[h, :, h] = np.transpose(tab, (1, 0, 2, 3))
        inv[:, :, h, :, h, :] = np.transpose(tab, (3, 0, 2, 1))
    return mid.reshape(2 * NZ, LANES), half.reshape(2 * NZ, LANES), inv.reshape(LANES, 2 * NZ)


def y_forward_table(kys):
    a = angle(kys, np.arange(NY), NY)
    return np.concatenate(split(np.cos(a) / math.sqrt(NY)) + split(np.sin(a) / math.sqrt(NY)), 0)


def x_forward_table():
    xs = np.arange(NX).reshape(GX, XL).T.reshape(NX)
    a = angle(TRIPLES, xs, NX)
    return np.concatenate(split(np.cos(a) / math.sqrt(NX)) + split(np.sin(a) / math.sqrt(NX)), 0)


def x_inverse_table():
    a = angle(np.arange(NX), TRIPLES, NX)
    return np.concatenate(split(np.cos(a)) + split(np.sin(a)), 1)


def y_inverse_table():
    a = angle(np.arange(NY), TRIPLES, NY)
    factor = 1.0 / math.sqrt(MX * MY * MZ)
    return np.concatenate(split(np.cos(a) * factor) + split(np.sin(a) * factor), 1)


def partial_tables():
    shift = (4 * np.arange(2)[:, None] + np.arange(2)[None, :]).reshape(4)
    lanes = 2 * (np.arange(LANES) // 64)
    a = (2.0 * np.pi / NX) * np.arange(MX)[:, None, None] * (shift[:, None] + lanes[None, :])[None]
    cos, sin = np.cos(a) / math.sqrt(NX), np.sin(a) / math.sqrt(NX)
    near = np.concatenate([cos, sin], 1).reshape(8 * MX, LANES)
    turn = np.concatenate([-sin, cos], 1).reshape(8 * MX, LANES)
    eighth = 2.0 * np.pi / 32 * np.arange(32)
    chip = np.repeat(np.stack([np.cos(eighth), np.sin(eighth)], 1), LANES, 1)
    parts = []
    for _ in range(3):
        parts.append(chip.astype(ml_dtypes.bfloat16))
        chip = chip - parts[-1].astype(np.float64)
    return near.astype(np.float32), turn.astype(np.float32), np.concatenate(parts, 0)


def expand_table():
    e = np.zeros((4, 2, 2, 8, 3, 2, 2, 8, C), ml_dtypes.bfloat16)
    for i in range(3):
        for r in range(2):
            for h in range(2):
                for c in range(8):
                    e[i, r, h, c, i, h, r, c, :] = 1.0
    return e.reshape(LANES, 6 * 2 * LANES)


def reorder_table():
    t = np.zeros((KZL, 2, C, 2, C, KZL), ml_dtypes.bfloat16)
    for k in range(KZL):
        for r in range(2):
            for c in range(C):
                t[k, r, c, r, c, k] = 1.0
    return t.reshape(LANES, LANES)


def dot(a, b):
    return jnp.dot(a, b, preferred_element_type=F32)


def dot_t(a, b):
    return lax.dot_general(a, b, (((1,), (1,)), ((), ())), preferred_element_type=F32)


def lane_of(shape):
    return lax.broadcasted_iota(jnp.int32, shape, len(shape) - 1)


def exchange(arrays, first):
    arrays = list(arrays)
    lane = lane_of(arrays[0].shape)
    bit = 1
    while bit < len(arrays):
        stride = first * bit
        clear = (lane & stride) == 0
        for i in range(len(arrays)):
            if i & bit:
                continue
            lo, hi = arrays[i], arrays[i | bit]
            arrays[i] = jnp.where(clear, lo, pltpu.roll(hi, stride, 1))
            arrays[i | bit] = jnp.where(clear, pltpu.roll(lo, LANES - stride, 1), hi)
        bit *= 2
    return arrays


def partner(v, stride):
    real = (lane_of(v.shape) & stride) == 0
    if stride == 64:
        return pltpu.roll(v, 64, 1), real
    return jnp.where(real, pltpu.roll(v, LANES - stride, 1), pltpu.roll(v, stride, 1)), real


def times_minus_i(v, stride):
    other, real = partner(v, stride)
    return jnp.where(real, other, -other)


def times_plus_i(v, stride):
    other, real = partner(v, stride)
    return jnp.where(real, -other, other)


def z_modes(even, odd, w_ref):
    modes = dot(even, w_ref[0:NZ, :]) + dot(odd, w_ref[NZ : 2 * NZ, :])
    modes = modes * (1.0 / math.sqrt(NZ))
    return [modes[i : i + ROWS] for i in range(0, modes.shape[0], ROWS)]


def expand_pointwise(pw):
    group = lax.broadcasted_iota(jnp.int32, (256, C), 0) // 16
    member = lax.broadcasted_iota(jnp.int32, (256, C), 1)
    one_hot = (group == member).astype(BF)
    wide = dot_t(dot_t(one_hot, pw).astype(BF), one_hot)
    r = lax.broadcasted_iota(jnp.int32, (256, 256), 0) % 16
    s = lax.broadcasted_iota(jnp.int32, (256, 256), 1) % 16
    return jnp.where(r == s, wide, 0.0).astype(BF)


def k1(field_ref, w_ref, pw_ref, out_ref, kron_ref, x_ref, t_ref, p_ref, sems):
    small = pltpu.make_async_copy(pw_ref, p_ref, sems.at[9])
    small.start()
    table = pltpu.make_async_copy(w_ref, t_ref, sems.at[8])
    table.start()
    copies = []
    for n in range(4):
        for h in range(2):
            part = pl.ds(8 * h + 2 * n, 2)
            copies.append(pltpu.make_async_copy(field_ref.at[part], x_ref.at[part], sems.at[2 * n + h]))
            copies[-1].start()
    small.wait()
    kron_ref[...] = expand_pointwise(p_ref[...])
    table.wait()
    modes = []
    for n in range(4):
        copies[2 * n].wait()
        copies[2 * n + 1].wait()
        even = x_ref[2 * n : 2 * n + 2].reshape(2 * ROWS, NZ)
        odd = x_ref[8 + 2 * n : 10 + 2 * n].reshape(2 * ROWS, NZ)
        modes += z_modes(even, odd, t_ref)
    for p, v in enumerate(exchange(modes, 1)):
        out_ref[p] = v.astype(BF)


def y_transform(full, ty_ref, stride):
    out = []
    for x in range(full.shape[1] // YL):
        rows = jnp.concatenate([full[p, YL * x : YL * x + YL, :] for p in range(GY)], 0).astype(BF)
        t = dot(ty_ref[...], rows)
        cos, sin = t[0:48] + t[48:96], t[96:144] + t[144:192]
        out.append(cos + times_minus_i(sin, stride))
    return out


def ky_of(value, quarter):
    t = value + OWNED * quarter
    return t - jnp.where(t >= 48, 48, 0) - jnp.where(t >= 96, 48, 0)


def place():
    return 2 * lax.axis_index("chip") + lax.axis_index("core")


def k2(in_ref, spec_ref, ty_ref, out_ref, scratch):
    for x, v in enumerate(y_transform(in_ref[...].astype(F32), ty_ref, 16)):
        parts = [v[0:16], v[16:32], v[32:48], jnp.zeros((16, LANES), F32)]
        for b, part in enumerate(exchange(parts, 32)):
            scratch[pl.ds(16 * b + x, 16, stride=64), :] = part
    quarter = place() % 4
    row = lax.broadcasted_iota(jnp.int32, (MY, OWNED), 0)
    mode = ky_of(lax.broadcasted_iota(jnp.int32, (MY, OWNED), 1), quarter)
    select = (mode == 3 * (row % 16) + row // 16).astype(BF)
    for b in range(KZL):
        moved = dot_t(select, spec_ref[pl.ds(b, 4 * LANES, stride=KZL), :].astype(BF))
        for k in range(4):
            for i in range(3):
                part = moved[16 * i : 16 * i + 16, LANES * k : LANES * k + LANES]
                scratch[pl.ds(16 * b + 4 + 4 * i + k, 16, stride=64), :] = part
    out_ref[...] = scratch[...].astype(BF)


def fold(arrays):
    lane = lane_of(arrays[0].shape)
    zero = jnp.zeros_like(arrays[0])
    arrays = arrays + [zero, zero]
    for stride in (64, 32, 16):
        n = len(arrays) // 2
        clear = (lane & stride) == 0
        merged = []
        for lo, hi in zip(arrays[:n], arrays[n:]):
            moved = jnp.where(clear, hi, lo)
            back = pltpu.roll(moved, stride, 1)
            if stride < 64:
                back = jnp.where(clear, pltpu.roll(moved, LANES - stride, 1), back)
            merged.append(jnp.where(clear, lo, hi) + back)
        arrays = merged
    return arrays[0]


def k3(in_ref, tx_ref, e_ref, tinv_ref, out_ref, scratch):
    a = place() // 4
    scratch[...] = in_ref[...].astype(F32)
    data = jnp.concatenate([scratch[pl.ds(x, GX, stride=16), :] for x in range(XL)], 0).astype(BF)
    t = dot(tx_ref[...], data)
    fwd = t[0:48] + t[48:96] + times_minus_i(t[96:144] + t[144:192], 16)
    fwd = fwd.astype(BF)
    source = (
        jnp.where(a >= 12, 1, 0),
        1 + jnp.where(a >= 8, 1, 0),
        2 + jnp.where(a >= 4, 1, 0),
    )

    def weights(i, k):
        at = 4 + 4 * i + k
        return jnp.concatenate(
            [scratch[pl.ds(16 * source[r] + at, 16, stride=64), :] for r in range(3)], 0
        )

    sums = []
    for i in range(3):
        real, imag = 0.0, 0.0
        for h in range(2):
            at = 256 * (2 * i + h)
            wide = dot(fwd, e_ref[:, at : at + 256])
            fr, fi = wide[:, 0:128], wide[:, 128:256]
            wr, wi = weights(i, h), weights(i, 2 + h)
            real += wr * fr - wi * fi
            imag += wr * fi + wi * fr
        sums += [real, imag]
    mixed = fold(sums)
    mixed = mixed.astype(BF)
    turned = times_plus_i(mixed.astype(F32), 16).astype(BF)
    moved = [
        jnp.where(lane_of(fwd.shape) >= 96, pltpu.roll(fwd.astype(F32), 96 - 32 * i, 1), 0.0)
        for i in range(3)
    ]
    moved = jnp.concatenate(moved, 0).astype(BF)
    row = lax.broadcasted_iota(jnp.int32, (NX, 3 * MX), 0)
    col = lax.broadcasted_iota(jnp.int32, (NX, 3 * MX), 1)
    owner = row // 4
    quarter = owner % 4
    back_one = jnp.where(quarter == 1, jnp.where(a >= 12, 1, 0), 0)
    back_one += jnp.where(quarter == 2, jnp.where(a >= 8, 1, 0), 0)
    r = jnp.minimum(quarter, 2) - back_one
    wanted = MX * (row % 4) + 16 * r + owner // 4
    select = (col == wanted).astype(BF)
    result = dot(tinv_ref[...], jnp.concatenate([mixed, mixed, turned, turned], 0))
    result += dot(select, moved)
    out_ref[...] = result.astype(BF)


def k4(in_ref, ty_ref, out_ref, fwd_ref, scratch):
    scratch[...] = in_ref[...].astype(F32)
    for x in range(XL):
        parts = [scratch[pl.ds(4 * b + x, 16, stride=16), :] for b in range(KZL)]
        parts = exchange(parts, 32)
        if x < 3:
            fwd_ref[16 * x : 16 * x + 16, :] = parts[3]
        v = jnp.concatenate(parts[0:3], 0)
        b = v.astype(BF)
        s = times_plus_i(v, 16).astype(BF)
        w = dot(ty_ref[...], jnp.concatenate([b, b, s, s], 0))
        for p in range(GY):
            out_ref[p, YL * x : YL * x + YL, :] = w[YL * p : YL * p + YL].astype(BF)


def slope(pre):
    square = pre * pre
    t = jnp.tanh(pre * (0.7978845608 + 0.7978845608 * 0.044715 * square))
    ramp = pre * (0.5 * 0.7978845608 + 1.5 * 0.7978845608 * 0.044715 * square)
    return (0.5 + 0.5 * t) + (1.0 - t * t) * ramp


def k5(waves_ref, field_ref, cot_ref, kron, w_ref, zt_ref, out_ref, grad):
    for n in range(ROWS // 16):
        rows = slice(16 * n, 16 * n + 16)
        parts = exchange([waves_ref[p, rows, :].astype(F32) for p in range(GY)], 1)
        waves = jnp.concatenate(parts, 0).astype(BF)
        x = field_ref[:, rows, :].reshape(C * 16, NZ)
        mapped = dot(kron[...], x)
        for h in range(2):
            pre = dot(waves, zt_ref[:, NZ * h : NZ * h + NZ]) + mapped[128 * h : 128 * h + 128]
            cot = cot_ref[8 * h : 8 * h + 8, rows, :].reshape(128, NZ).astype(F32)
            grad[8 * h : 8 * h + 8, rows, :] = (cot * slope(pre)).astype(BF).reshape(8, 16, NZ)
    even = grad[0:8].reshape(8 * ROWS, NZ)
    odd = grad[8:16].reshape(8 * ROWS, NZ)
    for p, v in enumerate(exchange(z_modes(even, odd, w_ref), 4)):
        for core, part in enumerate(exchange([v[0:48], v[48:96]], 64)):
            out_ref[8 * core + p] = part.astype(BF)


def k6(in_ref, ty_ref, near_ref, turn_ref, chip_ref, out_ref, factors):
    kx = lax.broadcasted_iota(jnp.int32, (MX, 96), 0)
    member = lax.broadcasted_iota(jnp.int32, (MX, 96), 1) % 32
    one_hot = (member == (kx * lax.axis_index("chip")) % 32).astype(BF)
    chip = dot(one_hot, chip_ref[...])
    for kx in range(MX):
        rows = slice(8 * kx, 8 * kx + 8)
        cos, sin = chip[kx : kx + 1, 0:128], chip[kx : kx + 1, 128:256]
        factors[rows, :] = near_ref[rows, :] * cos + turn_ref[rows, :] * sin
    full = in_ref[...].astype(F32)
    values = []
    for core in range(2):
        values += y_transform(full[8 * core : 8 * core + 8], ty_ref, 32)
    turned = [times_minus_i(v, 32) for v in values]
    low = lane_of((24, LANES)) < 64

    terms = values + turned
    for kx in range(0, MX, 2):
        rows = []
        for at in (8 * kx, 8 * kx + 8):
            acc = terms[0] * factors[at : at + 1, :]
            for n in range(1, 8):
                acc += terms[n] * factors[at + n : at + n + 1, :]
            even, odd = acc[0:24], acc[24:48]
            rows.append(jnp.where(low, even, odd) + pltpu.roll(jnp.where(low, odd, even), 64, 1))
        out_ref[24 * kx : 24 * kx + 48, :] = jnp.concatenate(rows, 0).astype(BF)


def k7(in_ref, fwd_ref, reorder_ref, spec_ref, mom_ref, out_ref, scratch, result, sems):
    quarter = place() % 4
    total = in_ref[0:72, :].astype(F32)
    for g in range(1, 16):
        total += in_ref[72 * g : 72 * g + 72, :].astype(F32)
    scratch[0:72, :] = total
    scratch[72:80, :] = jnp.zeros((8, LANES), F32)
    total = scratch[0:40, :] + scratch[36:76, :]
    row = lax.broadcasted_iota(jnp.int32, (2 * LANES, 120), 0)
    col = lax.broadcasted_iota(jnp.int32, (2 * LANES, 120), 1) % 40
    mode = row % LANES
    select = ((col == 18 * (row // LANES) + mode // 2) & (mode < OWNED)).astype(BF)
    parts = []
    for _ in range(3):
        parts.append(total.astype(BF).astype(F32))
        total = total - parts[-1]
    moved = dot(select, jnp.concatenate(parts, 0).astype(BF))
    first, second = moved[0:LANES], moved[LANES : 2 * LANES]
    odd = lax.broadcasted_iota(jnp.int32, (LANES, LANES), 0) % 2
    upper = lane_of((LANES, LANES)) // 64
    grads = jnp.where(upper == 0, first, second)
    other = jnp.where(upper == 0, pltpu.roll(first, 64, 1), pltpu.roll(second, 64, 1))
    grads = jnp.where(upper == odd, grads, other)
    row = lax.broadcasted_iota(jnp.int32, (LANES, MY), 0)
    col = lax.broadcasted_iota(jnp.int32, (LANES, MY), 1)
    hit = (ky_of(row, quarter) == 3 * (col % 16) + col // 16) & (row < OWNED)
    fwd = dot(hit.astype(BF), fwd_ref[...].astype(BF)).astype(BF)
    fwd = dot(fwd, reorder_ref[...])
    grads = grads.T[:, 0:OWNED]
    fwd = fwd.T[:, 0:OWNED]
    grad_r = jnp.concatenate([grads[0:32], grads[64:96]], 0)
    grad_i = jnp.concatenate([grads[32:64], grads[96:128]], 0)
    copies = []
    for c in range(C):
        fr = fwd[4 * c : 4 * c + 4]
        fi = fwd[64 + 4 * c : 68 + 4 * c]
        fr = jnp.concatenate([fr] * 16, 0)
        fi = jnp.concatenate([fi] * 16, 0)
        d_real = grad_r * fr + grad_i * fi
        d_imag = grad_i * fr - grad_r * fi
        result[0, c] = mom_ref[0, c] - 0.25 * (d_real + 2.0 * C * spec_ref[0, c])
        result[1, c] = mom_ref[1, c] - 0.25 * (d_imag + 2.0 * C * spec_ref[1, c])
        if c % 4 == 3:
            for r in range(2):
                part = pl.ds(c - 3, 4)
                copy = pltpu.make_async_copy(
                    result.at[r, part], out_ref.at[r, part], sems.at[2 * (c // 4) + r]
                )
                copy.start()
                copies.append(copy)
    for copy in copies:
        copy.wait()


def call(body, out, *args, scratch=(), hbm=(), out_space=pltpu.VMEM):
    specs = [
        pl.BlockSpec(memory_space=pltpu.HBM if i in hbm else pltpu.VMEM) for i in range(len(args))
    ]
    out_spec = pl.BlockSpec(memory_space=out_space)
    return pl.pallas_call(
        body,
        out_shape=out,
        in_specs=specs,
        out_specs=jax.tree.map(lambda _: out_spec, out),
        scratch_shapes=list(scratch),
        compiler_params=pltpu.CompilerParams(vmem_limit_bytes=40 * 1024 * 1024),
    )(*args)


def swap(value, axis):
    return lax.all_to_all(value, axis, split_axis=0, concat_axis=0, tiled=True)


def on_device(field, pointwise, spectral, momentum, cotangent):
    field = field.reshape(C, ROWS, NZ)
    cotangent = cotangent.reshape(C, ROWS, NZ)
    spectral = jnp.transpose(spectral, (1, 2, 3, 4, 0))
    momentum = jnp.transpose(momentum, (1, 2, 3, 4, 0))
    z_mid, z_half, z_inv = [jnp.asarray(t) for t in z_tables()]
    zshape = jax.ShapeDtypeStruct((GY, ROWS, LANES), BF)

    zmodes, kron = call(
        k1,
        (zshape, jax.ShapeDtypeStruct((256, 256), BF)),
        pltpu.with_memory_space_constraint(field, pltpu.HBM),
        pltpu.with_memory_space_constraint(z_mid, pltpu.HBM),
        pltpu.with_memory_space_constraint(pointwise, pltpu.HBM),
        hbm=(0, 1, 2),
        scratch=[
            pltpu.VMEM((C, ROWS, NZ), BF),
            pltpu.VMEM((2 * NZ, LANES), BF),
            pltpu.VMEM((C, C), BF),
            pltpu.SemaphoreType.DMA((10,)),
        ],
    )
    zmodes = swap(zmodes, "gy")
    sent = call(
        k2,
        jax.ShapeDtypeStruct((GX * 16, LANES), BF),
        zmodes,
        spectral.reshape(2 * C * C * KZL, OWNED),
        jnp.asarray(y_forward_table(TRIPLES)),
        scratch=[pltpu.VMEM((GX * 16, LANES), F32)],
    )
    got = swap(sent.reshape(GX, 16, LANES), GXS).reshape(GX * 16, LANES)
    sent = call(
        k3,
        jax.ShapeDtypeStruct((NX, LANES), BF),
        got,
        jnp.asarray(x_forward_table()),
        jnp.asarray(expand_table()),
        jnp.asarray(x_inverse_table()),
        scratch=[pltpu.VMEM((GX * 16, LANES), F32)],
    )
    back = swap(sent.reshape(GX, XL, LANES), GXS).reshape(NX, LANES)
    waves, fwd = call(
        k4,
        (zshape, jax.ShapeDtypeStruct((MY, LANES), F32)),
        back,
        jnp.asarray(y_inverse_table()),
        scratch=[pltpu.VMEM((NX, LANES), F32)],
    )
    zgrads = call(
        k5,
        jax.ShapeDtypeStruct((2 * GY, ROWS // 2, LANES), BF),
        swap(waves, "gy"),
        field,
        cotangent,
        kron,
        z_half,
        z_inv,
        scratch=[pltpu.VMEM((C, ROWS, NZ), BF)],
    )
    partial = call(
        k6,
        jax.ShapeDtypeStruct((MX * MY // 2, LANES), BF),
        swap(zgrads, ("core", "gy")),
        jnp.asarray(y_forward_table(PAIRS)),
        *[jnp.asarray(t) for t in partial_tables()],
        scratch=[pltpu.VMEM((8 * MX, LANES), F32)],
    )
    partial = swap(partial.reshape(GX, OWNED // 4, 2, LANES), GXS).reshape(MX * MY // 2, LANES)
    result = call(
        k7,
        jax.ShapeDtypeStruct((2, C, C * KZL, OWNED), F32),
        partial,
        fwd,
        jnp.asarray(reorder_table()),
        spectral.reshape(2, C, C * KZL, OWNED),
        momentum.reshape(2, C, C * KZL, OWNED),
        scratch=[
            pltpu.VMEM((80, LANES), F32),
            pltpu.VMEM((2, C, C * KZL, OWNED), F32),
            pltpu.SemaphoreType.DMA((8,)),
        ],
        out_space=pltpu.HBM,
    )
    result = result.reshape(2, C, C, KZL, OWNED)
    return jnp.transpose(result, (4, 0, 1, 2, 3))


def solution(mesh):
    chips = jax.sharding.Mesh(mesh.devices.reshape(GX // 2, 2, GY), ("chip", "core", "gy"))
    in_specs = (
        P(None, GXS, "gy", None),
        P(),
        P(GXS, None, None, None, "gy"),
        P(GXS, None, None, None, "gy"),
        P(None, GXS, "gy", None),
    )
    out_specs = P(GXS, None, None, None, "gy")
    return jax.shard_map(
        on_device, mesh=chips, in_specs=in_specs, out_specs=out_specs, check_vma=False
    )
```

```python
import math

import jax
import jax.numpy as jnp
import ml_dtypes
import numpy as np
from jax import lax
from jax.experimental import pallas as pl
from jax.experimental.pallas import tpu as pltpu
from jax.sharding import PartitionSpec as P

C = 16
MX = 48
MY = 48
MZ = 32
NX = 256
NY = 192
NZ = 512
GX = 64
GY = 8
XL = NX // GX
YL = NY // GY
KZL = MZ // GY
ROWS = XL * YL
BF = jnp.bfloat16
F32 = jnp.float32
LANES = 128
OWNED = MX * MY // GX
GXS = ("chip", "core")
CORE_FIRST = ("core", "chip")
ORDER = np.arange(GX).reshape(GX // 2, 2).T.reshape(GX)
TRIPLES = np.arange(48).reshape(16, 3).T.reshape(48)
PAIRS = np.arange(48).reshape(24, 2).T.reshape(48)


def angle(a, b, n):
    return (2.0 * np.pi / n) * ((np.asarray(a)[:, None] * np.asarray(b)[None, :]) % n).astype(np.float64)


def split(table):
    table = np.asarray(table, np.float64)
    high = table.astype(ml_dtypes.bfloat16)
    low = (table - high.astype(np.float64)).astype(ml_dtypes.bfloat16)
    return high, low


def z_tables():
    a = angle(np.arange(NZ), np.arange(MZ), NZ).astype(np.float32)
    tab = np.stack([np.cos(a), -np.sin(a)], 0).astype(ml_dtypes.bfloat16)
    tab = tab.reshape(2, NZ, GY, KZL)
    mid = np.zeros((2, NZ, KZL, 2, 2, GY), ml_dtypes.bfloat16)
    half = np.zeros((2, NZ, 2, 2, GY, KZL), ml_dtypes.bfloat16)
    inv = np.zeros((KZL, 2, 2, GY, 2, NZ), ml_dtypes.bfloat16)
    for h in range(2):
        mid[h, :, :, :, h] = np.transpose(tab, (1, 3, 0, 2))
        half[h, :, h] = np.transpose(tab, (1, 0, 2, 3))
        inv[:, :, h, :, h, :] = np.transpose(tab, (3, 0, 2, 1))
    return mid.reshape(2 * NZ, LANES), half.reshape(2 * NZ, LANES), inv.reshape(LANES, 2 * NZ)


def y_forward_table(kys):
    a = angle(kys, np.arange(NY), NY)
    return np.concatenate(split(np.cos(a) / math.sqrt(NY)) + split(np.sin(a) / math.sqrt(NY)), 0)


def x_forward_table():
    xs = np.arange(NX).reshape(GX, XL)[ORDER].T.reshape(NX)
    a = angle(TRIPLES, xs, NX)
    return np.concatenate(split(np.cos(a) / math.sqrt(NX)) + split(np.sin(a) / math.sqrt(NX)), 0)


def x_inverse_table():
    a = angle(np.arange(NX).reshape(GX, XL)[ORDER].reshape(NX), TRIPLES, NX)
    return np.concatenate(split(np.cos(a)) + split(np.sin(a)), 1)


def y_inverse_table():
    a = angle(np.arange(NY), TRIPLES, NY)
    factor = 1.0 / math.sqrt(MX * MY * MZ)
    return np.concatenate(split(np.cos(a) * factor) + split(np.sin(a) * factor), 1)


def partial_tables():
    shift = (4 * np.arange(2)[:, None] + np.arange(2)[None, :]).reshape(4)
    lanes = 2 * (np.arange(LANES) // 64)
    a = (2.0 * np.pi / NX) * np.arange(MX)[:, None, None] * (shift[:, None] + lanes[None, :])[None]
    cos, sin = np.cos(a) / math.sqrt(NX), np.sin(a) / math.sqrt(NX)
    near = np.concatenate([cos, sin], 1).reshape(8 * MX, LANES)
    turn = np.concatenate([-sin, cos], 1).reshape(8 * MX, LANES)
    eighth = 2.0 * np.pi / 32 * np.arange(32)
    chip = np.repeat(np.stack([np.cos(eighth), np.sin(eighth)], 1), LANES, 1)
    parts = []
    for _ in range(3):
        parts.append(chip.astype(ml_dtypes.bfloat16))
        chip = chip - parts[-1].astype(np.float64)
    return near.astype(np.float32), turn.astype(np.float32), np.concatenate(parts, 0)


def expand_table():
    e = np.zeros((4, 2, 2, 8, 3, 2, 2, 8, C), ml_dtypes.bfloat16)
    for i in range(3):
        for r in range(2):
            for h in range(2):
                for c in range(8):
                    e[i, r, h, c, i, h, r, c, :] = 1.0
    return e.reshape(LANES, 6 * 2 * LANES)


def reorder_table():
    t = np.zeros((KZL, 2, C, 2, C, KZL), ml_dtypes.bfloat16)
    for k in range(KZL):
        for r in range(2):
            for c in range(C):
                t[k, r, c, r, c, k] = 1.0
    return t.reshape(LANES, LANES)


def dot(a, b):
    return jnp.dot(a, b, preferred_element_type=F32)


def dot_t(a, b):
    return lax.dot_general(a, b, (((1,), (1,)), ((), ())), preferred_element_type=F32)


def lane_of(shape):
    return lax.broadcasted_iota(jnp.int32, shape, len(shape) - 1)


def exchange(arrays, first):
    arrays = list(arrays)
    lane = lane_of(arrays[0].shape)
    bit = 1
    while bit < len(arrays):
        stride = first * bit
        clear = (lane & stride) == 0
        for i in range(len(arrays)):
            if i & bit:
                continue
            lo, hi = arrays[i], arrays[i | bit]
            arrays[i] = jnp.where(clear, lo, pltpu.roll(hi, stride, 1))
            arrays[i | bit] = jnp.where(clear, pltpu.roll(lo, LANES - stride, 1), hi)
        bit *= 2
    return arrays


def partner(v, stride):
    real = (lane_of(v.shape) & stride) == 0
    if stride == 64:
        return pltpu.roll(v, 64, 1), real
    return jnp.where(real, pltpu.roll(v, LANES - stride, 1), pltpu.roll(v, stride, 1)), real


def times_minus_i(v, stride):
    other, real = partner(v, stride)
    return jnp.where(real, other, -other)


def times_plus_i(v, stride):
    other, real = partner(v, stride)
    return jnp.where(real, -other, other)


def z_modes(even, odd, w_ref):
    modes = dot(even, w_ref[0:NZ, :]) + dot(odd, w_ref[NZ : 2 * NZ, :])
    modes = modes * (1.0 / math.sqrt(NZ))
    return [modes[i : i + ROWS] for i in range(0, modes.shape[0], ROWS)]


def expand_pointwise(pw):
    group = lax.broadcasted_iota(jnp.int32, (256, C), 0) // 16
    member = lax.broadcasted_iota(jnp.int32, (256, C), 1)
    one_hot = (group == member).astype(BF)
    wide = dot_t(dot_t(one_hot, pw).astype(BF), one_hot)
    r = lax.broadcasted_iota(jnp.int32, (256, 256), 0) % 16
    s = lax.broadcasted_iota(jnp.int32, (256, 256), 1) % 16
    return jnp.where(r == s, wide, 0.0).astype(BF)


def k1(field_ref, w_ref, pw_ref, out_ref, kron_ref, x_ref, t_ref, p_ref, sems):
    small = pltpu.make_async_copy(pw_ref, p_ref, sems.at[9])
    small.start()
    table = pltpu.make_async_copy(w_ref, t_ref, sems.at[8])
    table.start()
    copies = []
    for n in range(4):
        for h in range(2):
            part = pl.ds(8 * h + 2 * n, 2)
            copies.append(pltpu.make_async_copy(field_ref.at[part], x_ref.at[part], sems.at[2 * n + h]))
            copies[-1].start()
    small.wait()
    kron_ref[...] = expand_pointwise(p_ref[...])
    table.wait()
    modes = []
    for n in range(4):
        copies[2 * n].wait()
        copies[2 * n + 1].wait()
        even = x_ref[2 * n : 2 * n + 2].reshape(2 * ROWS, NZ)
        odd = x_ref[8 + 2 * n : 10 + 2 * n].reshape(2 * ROWS, NZ)
        modes += z_modes(even, odd, t_ref)
    for p, v in enumerate(exchange(modes, 1)):
        out_ref[p] = v.astype(BF)


def y_transform(full, ty_ref, stride):
    out = []
    for x in range(full.shape[1] // YL):
        rows = jnp.concatenate([full[p, YL * x : YL * x + YL, :] for p in range(GY)], 0).astype(BF)
        t = dot(ty_ref[...], rows)
        cos, sin = t[0:48] + t[48:96], t[96:144] + t[144:192]
        out.append(cos + times_minus_i(sin, stride))
    return out


def ky_of(value, quarter):
    t = value + OWNED * quarter
    return t - jnp.where(t >= 48, 48, 0) - jnp.where(t >= 96, 48, 0)


def place():
    return 2 * lax.axis_index("chip") + lax.axis_index("core")


def first_of(member):
    return 32 * (member % 2) + member // 2


def k2(in_ref, spec_ref, ty_ref, out_ref, scratch):
    for x, v in enumerate(y_transform(in_ref[...].astype(F32), ty_ref, 16)):
        parts = [v[0:16], v[16:32], v[32:48], jnp.zeros((16, LANES), F32)]
        for b, part in enumerate(exchange(parts, 32)):
            scratch[pl.ds(16 * first_of(b) + x, 16, stride=32), :] = part
    quarter = place() % 4
    row = lax.broadcasted_iota(jnp.int32, (MY, OWNED), 0)
    mode = ky_of(lax.broadcasted_iota(jnp.int32, (MY, OWNED), 1), quarter)
    select = (mode == 3 * (row % 16) + row // 16).astype(BF)
    for b in range(KZL):
        moved = dot_t(select, spec_ref[pl.ds(b, 4 * LANES, stride=KZL), :].astype(BF))
        for k in range(4):
            for i in range(3):
                part = moved[16 * i : 16 * i + 16, LANES * k : LANES * k + LANES]
                scratch[pl.ds(16 * first_of(b) + 4 + 4 * i + k, 16, stride=32), :] = part
    out_ref[...] = scratch[...].astype(BF)


def fold(arrays):
    lane = lane_of(arrays[0].shape)
    zero = jnp.zeros_like(arrays[0])
    arrays = arrays + [zero, zero]
    for stride in (64, 32, 16):
        n = len(arrays) // 2
        clear = (lane & stride) == 0
        merged = []
        for lo, hi in zip(arrays[:n], arrays[n:]):
            moved = jnp.where(clear, hi, lo)
            back = pltpu.roll(moved, stride, 1)
            if stride < 64:
                back = jnp.where(clear, pltpu.roll(moved, LANES - stride, 1), back)
            merged.append(jnp.where(clear, lo, hi) + back)
        arrays = merged
    return arrays[0]


def k3(in_ref, tx_ref, e_ref, tinv_ref, out_ref, scratch):
    a = place() // 4
    scratch[...] = in_ref[...].astype(F32)
    data = jnp.concatenate([scratch[pl.ds(x, GX, stride=16), :] for x in range(XL)], 0).astype(BF)
    t = dot(tx_ref[...], data)
    fwd = t[0:48] + t[48:96] + times_minus_i(t[96:144] + t[144:192], 16)
    fwd = fwd.astype(BF)
    source = (
        jnp.where(a >= 12, 1, 0),
        1 + jnp.where(a >= 8, 1, 0),
        2 + jnp.where(a >= 4, 1, 0),
    )

    def weights(i, k):
        at = 4 + 4 * i + k
        return jnp.concatenate(
            [scratch[pl.ds(16 * first_of(source[r]) + at, 16, stride=32), :] for r in range(3)], 0
        )

    sums = []
    for i in range(3):
        real, imag = 0.0, 0.0
        for h in range(2):
            at = 256 * (2 * i + h)
            wide = dot(fwd, e_ref[:, at : at + 256])
            fr, fi = wide[:, 0:128], wide[:, 128:256]
            wr, wi = weights(i, h), weights(i, 2 + h)
            real += wr * fr - wi * fi
            imag += wr * fi + wi * fr
        sums += [real, imag]
    mixed = fold(sums)
    mixed = mixed.astype(BF)
    turned = times_plus_i(mixed.astype(F32), 16).astype(BF)
    moved = [
        jnp.where(lane_of(fwd.shape) >= 96, pltpu.roll(fwd.astype(F32), 96 - 32 * i, 1), 0.0)
        for i in range(3)
    ]
    moved = jnp.concatenate(moved, 0).astype(BF)
    row = lax.broadcasted_iota(jnp.int32, (NX, 3 * MX), 0)
    col = lax.broadcasted_iota(jnp.int32, (NX, 3 * MX), 1)
    owner = 2 * (row // 4 % 32) + row // 128
    quarter = owner % 4
    back_one = jnp.where(quarter == 1, jnp.where(a >= 12, 1, 0), 0)
    back_one += jnp.where(quarter == 2, jnp.where(a >= 8, 1, 0), 0)
    r = jnp.minimum(quarter, 2) - back_one
    wanted = MX * (row % 4) + 16 * r + owner // 4
    select = (col == wanted).astype(BF)
    result = dot(tinv_ref[...], jnp.concatenate([mixed, mixed, turned, turned], 0))
    result += dot(select, moved)
    out_ref[...] = result.astype(BF)


def k4(in_ref, ty_ref, out_ref, fwd_ref, scratch):
    scratch[...] = in_ref[...].astype(F32)
    for x in range(XL):
        parts = [scratch[pl.ds(4 * first_of(b) + x, 16, stride=8), :] for b in range(KZL)]
        parts = exchange(parts, 32)
        if x < 3:
            fwd_ref[16 * x : 16 * x + 16, :] = parts[3]
        v = jnp.concatenate(parts[0:3], 0)
        b = v.astype(BF)
        s = times_plus_i(v, 16).astype(BF)
        w = dot(ty_ref[...], jnp.concatenate([b, b, s, s], 0))
        for p in range(GY):
            out_ref[p, YL * x : YL * x + YL, :] = w[YL * p : YL * p + YL].astype(BF)


def slope(pre):
    square = pre * pre
    t = jnp.tanh(pre * (0.7978845608 + 0.7978845608 * 0.044715 * square))
    ramp = pre * (0.5 * 0.7978845608 + 1.5 * 0.7978845608 * 0.044715 * square)
    return (0.5 + 0.5 * t) + (1.0 - t * t) * ramp


def k5(waves_ref, field_ref, cot_ref, kron, w_ref, zt_ref, out_ref, grad):
    for n in range(ROWS // 16):
        rows = slice(16 * n, 16 * n + 16)
        parts = exchange([waves_ref[p, rows, :].astype(F32) for p in range(GY)], 1)
        waves = jnp.concatenate(parts, 0).astype(BF)
        x = field_ref[:, rows, :].reshape(C * 16, NZ)
        mapped = dot(kron[...], x)
        for h in range(2):
            pre = dot(waves, zt_ref[:, NZ * h : NZ * h + NZ]) + mapped[128 * h : 128 * h + 128]
            cot = cot_ref[8 * h : 8 * h + 8, rows, :].reshape(128, NZ).astype(F32)
            grad[8 * h : 8 * h + 8, rows, :] = (cot * slope(pre)).astype(BF).reshape(8, 16, NZ)
    even = grad[0:8].reshape(8 * ROWS, NZ)
    odd = grad[8:16].reshape(8 * ROWS, NZ)
    for p, v in enumerate(exchange(z_modes(even, odd, w_ref), 4)):
        for core, part in enumerate(exchange([v[0:48], v[48:96]], 64)):
            out_ref[8 * core + p] = part.astype(BF)


def k6(in_ref, ty_ref, near_ref, turn_ref, chip_ref, out_ref, factors):
    kx = lax.broadcasted_iota(jnp.int32, (MX, 96), 0)
    member = lax.broadcasted_iota(jnp.int32, (MX, 96), 1) % 32
    one_hot = (member == (kx * lax.axis_index("chip")) % 32).astype(BF)
    chip = dot(one_hot, chip_ref[...])
    for kx in range(MX):
        rows = slice(8 * kx, 8 * kx + 8)
        cos, sin = chip[kx : kx + 1, 0:128], chip[kx : kx + 1, 128:256]
        factors[rows, :] = near_ref[rows, :] * cos + turn_ref[rows, :] * sin
    full = in_ref[...].astype(F32)
    values = []
    for core in range(2):
        values += y_transform(full[8 * core : 8 * core + 8], ty_ref, 32)
    turned = [times_minus_i(v, 32) for v in values]
    low = lane_of((24, LANES)) < 64

    terms = values + turned
    for kx in range(0, MX, 2):
        rows = []
        for at in (8 * kx, 8 * kx + 8):
            acc = terms[0] * factors[at : at + 1, :]
            for n in range(1, 8):
                acc += terms[n] * factors[at + n : at + n + 1, :]
            even, odd = acc[0:24], acc[24:48]
            rows.append(jnp.where(low, even, odd) + pltpu.roll(jnp.where(low, odd, even), 64, 1))
        out_ref[24 * kx : 24 * kx + 48, :] = jnp.concatenate(rows, 0).astype(BF)


def k7(in_ref, fwd_ref, reorder_ref, spec_ref, mom_ref, out_ref, scratch, result, sems):
    quarter = place() % 4
    total = in_ref[0:72, :].astype(F32)
    for g in range(1, 16):
        total += in_ref[72 * g : 72 * g + 72, :].astype(F32)
    scratch[0:72, :] = total
    scratch[72:80, :] = jnp.zeros((8, LANES), F32)
    total = scratch[0:40, :] + scratch[36:76, :]
    row = lax.broadcasted_iota(jnp.int32, (2 * LANES, 120), 0)
    col = lax.broadcasted_iota(jnp.int32, (2 * LANES, 120), 1) % 40
    mode = row % LANES
    select = ((col == 18 * (row // LANES) + mode // 2) & (mode < OWNED)).astype(BF)
    parts = []
    for _ in range(3):
        parts.append(total.astype(BF).astype(F32))
        total = total - parts[-1]
    moved = dot(select, jnp.concatenate(parts, 0).astype(BF))
    first, second = moved[0:LANES], moved[LANES : 2 * LANES]
    odd = lax.broadcasted_iota(jnp.int32, (LANES, LANES), 0) % 2
    upper = lane_of((LANES, LANES)) // 64
    grads = jnp.where(upper == 0, first, second)
    other = jnp.where(upper == 0, pltpu.roll(first, 64, 1), pltpu.roll(second, 64, 1))
    grads = jnp.where(upper == odd, grads, other)
    row = lax.broadcasted_iota(jnp.int32, (LANES, MY), 0)
    col = lax.broadcasted_iota(jnp.int32, (LANES, MY), 1)
    hit = (ky_of(row, quarter) == 3 * (col % 16) + col // 16) & (row < OWNED)
    fwd = dot(hit.astype(BF), fwd_ref[...].astype(BF)).astype(BF)
    fwd = dot(fwd, reorder_ref[...])
    grads = grads.T[:, 0:OWNED]
    fwd = fwd.T[:, 0:OWNED]
    grad_r = jnp.concatenate([grads[0:32], grads[64:96]], 0)
    grad_i = jnp.concatenate([grads[32:64], grads[96:128]], 0)
    copies = []
    for c in range(C):
        fr = fwd[4 * c : 4 * c + 4]
        fi = fwd[64 + 4 * c : 68 + 4 * c]
        fr = jnp.concatenate([fr] * 16, 0)
        fi = jnp.concatenate([fi] * 16, 0)
        d_real = grad_r * fr + grad_i * fi
        d_imag = grad_i * fr - grad_r * fi
        result[0, c] = mom_ref[0, c] - 0.25 * (d_real + 2.0 * C * spec_ref[0, c])
        result[1, c] = mom_ref[1, c] - 0.25 * (d_imag + 2.0 * C * spec_ref[1, c])
        if c % 4 == 3:
            for r in range(2):
                part = pl.ds(c - 3, 4)
                copy = pltpu.make_async_copy(
                    result.at[r, part], out_ref.at[r, part], sems.at[2 * (c // 4) + r]
                )
                copy.start()
                copies.append(copy)
    for copy in copies:
        copy.wait()


def call(body, out, *args, scratch=(), hbm=(), out_space=pltpu.VMEM):
    specs = [
        pl.BlockSpec(memory_space=pltpu.HBM if i in hbm else pltpu.VMEM) for i in range(len(args))
    ]
    out_spec = pl.BlockSpec(memory_space=out_space)
    return pl.pallas_call(
        body,
        out_shape=out,
        in_specs=specs,
        out_specs=jax.tree.map(lambda _: out_spec, out),
        scratch_shapes=list(scratch),
        compiler_params=pltpu.CompilerParams(vmem_limit_bytes=40 * 1024 * 1024),
    )(*args)


def swap(value, axis):
    return lax.all_to_all(value, axis, split_axis=0, concat_axis=0, tiled=True)


def on_device(field, pointwise, spectral, momentum, cotangent):
    field = field.reshape(C, ROWS, NZ)
    cotangent = cotangent.reshape(C, ROWS, NZ)
    spectral = jnp.transpose(spectral, (1, 2, 3, 4, 0))
    momentum = jnp.transpose(momentum, (1, 2, 3, 4, 0))
    z_mid, z_half, z_inv = [jnp.asarray(t) for t in z_tables()]
    zshape = jax.ShapeDtypeStruct((GY, ROWS, LANES), BF)

    zmodes, kron = call(
        k1,
        (zshape, jax.ShapeDtypeStruct((256, 256), BF)),
        pltpu.with_memory_space_constraint(field, pltpu.HBM),
        pltpu.with_memory_space_constraint(z_mid, pltpu.HBM),
        pltpu.with_memory_space_constraint(pointwise, pltpu.HBM),
        hbm=(0, 1, 2),
        scratch=[
            pltpu.VMEM((C, ROWS, NZ), BF),
            pltpu.VMEM((2 * NZ, LANES), BF),
            pltpu.VMEM((C, C), BF),
            pltpu.SemaphoreType.DMA((10,)),
        ],
    )
    zmodes = swap(zmodes, "gy")
    sent = call(
        k2,
        jax.ShapeDtypeStruct((GX * 16, LANES), BF),
        zmodes,
        spectral.reshape(2 * C * C * KZL, OWNED),
        jnp.asarray(y_forward_table(TRIPLES)),
        scratch=[pltpu.VMEM((GX * 16, LANES), F32)],
    )
    got = swap(sent.reshape(GX, 16, LANES), CORE_FIRST).reshape(GX * 16, LANES)
    sent = call(
        k3,
        jax.ShapeDtypeStruct((NX, LANES), BF),
        got,
        jnp.asarray(x_forward_table()),
        jnp.asarray(expand_table()),
        jnp.asarray(x_inverse_table()),
        scratch=[pltpu.VMEM((GX * 16, LANES), F32)],
    )
    back = swap(sent.reshape(GX, XL, LANES), CORE_FIRST).reshape(NX, LANES)
    waves, fwd = call(
        k4,
        (zshape, jax.ShapeDtypeStruct((MY, LANES), F32)),
        back,
        jnp.asarray(y_inverse_table()),
        scratch=[pltpu.VMEM((NX, LANES), F32)],
    )
    zgrads = call(
        k5,
        jax.ShapeDtypeStruct((2 * GY, ROWS // 2, LANES), BF),
        swap(waves, "gy"),
        field,
        cotangent,
        kron,
        z_half,
        z_inv,
        scratch=[pltpu.VMEM((C, ROWS, NZ), BF)],
    )
    partial = call(
        k6,
        jax.ShapeDtypeStruct((MX * MY // 2, LANES), BF),
        swap(zgrads, ("core", "gy")),
        jnp.asarray(y_forward_table(PAIRS)),
        *[jnp.asarray(t) for t in partial_tables()],
        scratch=[pltpu.VMEM((8 * MX, LANES), F32)],
    )
    partial = swap(partial.reshape(GX, OWNED // 4, 2, LANES), GXS).reshape(MX * MY // 2, LANES)
    result = call(
        k7,
        jax.ShapeDtypeStruct((2, C, C * KZL, OWNED), F32),
        partial,
        fwd,
        jnp.asarray(reorder_table()),
        spectral.reshape(2, C, C * KZL, OWNED),
        momentum.reshape(2, C, C * KZL, OWNED),
        scratch=[
            pltpu.VMEM((80, LANES), F32),
            pltpu.VMEM((2, C, C * KZL, OWNED), F32),
            pltpu.SemaphoreType.DMA((8,)),
        ],
        out_space=pltpu.HBM,
    )
    result = result.reshape(2, C, C, KZL, OWNED)
    return jnp.transpose(result, (4, 0, 1, 2, 3))


def solution(mesh):
    chips = jax.sharding.Mesh(mesh.devices.reshape(GX // 2, 2, GY), ("chip", "core", "gy"))
    in_specs = (
        P(None, GXS, "gy", None),
        P(),
        P(GXS, None, None, None, "gy"),
        P(GXS, None, None, None, "gy"),
        P(None, GXS, "gy", None),
    )
    out_specs = P(GXS, None, None, None, "gy")
    return jax.shard_map(
        on_device, mesh=chips, in_specs=in_specs, out_specs=out_specs, check_vma=False
    )
```

```python
import math

import jax
import jax.numpy as jnp
import ml_dtypes
import numpy as np
from jax import lax
from jax.experimental import pallas as pl
from jax.experimental.pallas import tpu as pltpu
from jax.sharding import PartitionSpec as P

C = 16
MX = 48
MY = 48
MZ = 32
NX = 256
NY = 192
NZ = 512
GX = 64
GY = 8
XL = NX // GX
YL = NY // GY
KZL = MZ // GY
ROWS = XL * YL
BF = jnp.bfloat16
F32 = jnp.float32
LANES = 128
OWNED = MX * MY // GX
GXS = ("chip", "core")
CORE_FIRST = ("core", "chip")
ORDER = np.arange(GX).reshape(GX // 2, 2).T.reshape(GX)
TRIPLES = np.arange(48).reshape(16, 3).T.reshape(48)
PAIRS = np.arange(48).reshape(24, 2).T.reshape(48)


def angle(a, b, n):
    return (2.0 * np.pi / n) * ((np.asarray(a)[:, None] * np.asarray(b)[None, :]) % n).astype(np.float64)


def split(table):
    table = np.asarray(table, np.float64)
    high = table.astype(ml_dtypes.bfloat16)
    low = (table - high.astype(np.float64)).astype(ml_dtypes.bfloat16)
    return high, low


def z_tables():
    a = angle(np.arange(NZ), np.arange(MZ), NZ).astype(np.float32)
    tab = np.stack([np.cos(a), -np.sin(a)], 0).astype(ml_dtypes.bfloat16)
    tab = tab.reshape(2, NZ, GY, KZL)
    mid = np.zeros((2, NZ, KZL, 2, 2, GY), ml_dtypes.bfloat16)
    half = np.zeros((2, NZ, 2, 2, GY, KZL), ml_dtypes.bfloat16)
    inv = np.zeros((KZL, 2, 2, GY, 2, NZ), ml_dtypes.bfloat16)
    for h in range(2):
        mid[h, :, :, :, h] = np.transpose(tab, (1, 3, 0, 2))
        half[h, :, h] = np.transpose(tab, (1, 0, 2, 3))
        inv[:, :, h, :, h, :] = np.transpose(tab, (3, 0, 2, 1))
    return mid.reshape(2 * NZ, LANES), half.reshape(2 * NZ, LANES), inv.reshape(LANES, 2 * NZ)


def y_forward_table(kys):
    a = angle(kys, np.arange(NY), NY)
    return np.concatenate(split(np.cos(a) / math.sqrt(NY)) + split(np.sin(a) / math.sqrt(NY)), 0)


def x_forward_table():
    xs = np.arange(NX).reshape(GX, XL)[ORDER].T.reshape(NX)
    a = angle(TRIPLES, xs, NX)
    return np.concatenate(split(np.cos(a) / math.sqrt(NX)) + split(np.sin(a) / math.sqrt(NX)), 0)


def x_inverse_table():
    a = angle(np.arange(NX).reshape(GX, XL)[ORDER].reshape(NX), TRIPLES, NX)
    return np.concatenate(split(np.cos(a)) + split(np.sin(a)), 1)


def y_inverse_table():
    a = angle(np.arange(NY), TRIPLES, NY)
    factor = 1.0 / math.sqrt(MX * MY * MZ)
    return np.concatenate(split(np.cos(a) * factor) + split(np.sin(a) * factor), 1)


def partial_tables():
    shift = (4 * np.arange(2)[:, None] + np.arange(2)[None, :]).reshape(4)
    lanes = 2 * (np.arange(LANES) // 64)
    a = (2.0 * np.pi / NX) * np.arange(MX)[:, None, None] * (shift[:, None] + lanes[None, :])[None]
    cos, sin = np.cos(a) / math.sqrt(NX), np.sin(a) / math.sqrt(NX)
    near = np.concatenate([cos, sin], 1).reshape(8 * MX, LANES)
    turn = np.concatenate([-sin, cos], 1).reshape(8 * MX, LANES)
    eighth = 2.0 * np.pi / 32 * np.arange(32)
    chip = np.repeat(np.stack([np.cos(eighth), np.sin(eighth)], 1), LANES, 1)
    parts = []
    for _ in range(3):
        parts.append(chip.astype(ml_dtypes.bfloat16))
        chip = chip - parts[-1].astype(np.float64)
    return near.astype(np.float32), turn.astype(np.float32), np.concatenate(parts, 0)


def expand_table():
    e = np.zeros((4, 2, 2, 8, 3, 2, 2, 8, C), ml_dtypes.bfloat16)
    for i in range(3):
        for r in range(2):
            for h in range(2):
                for c in range(8):
                    e[i, r, h, c, i, h, r, c, :] = 1.0
    return e.reshape(LANES, 6 * 2 * LANES)


def reorder_table():
    t = np.zeros((KZL, 2, C, 2, C, KZL), ml_dtypes.bfloat16)
    for k in range(KZL):
        for r in range(2):
            for c in range(C):
                t[k, r, c, r, c, k] = 1.0
    return t.reshape(LANES, LANES)


def dot(a, b):
    return jnp.dot(a, b, preferred_element_type=F32)


def dot_t(a, b):
    return lax.dot_general(a, b, (((1,), (1,)), ((), ())), preferred_element_type=F32)


def lane_of(shape):
    return lax.broadcasted_iota(jnp.int32, shape, len(shape) - 1)


def exchange(arrays, first):
    arrays = list(arrays)
    lane = lane_of(arrays[0].shape)
    bit = 1
    while bit < len(arrays):
        stride = first * bit
        clear = (lane & stride) == 0
        for i in range(len(arrays)):
            if i & bit:
                continue
            lo, hi = arrays[i], arrays[i | bit]
            arrays[i] = jnp.where(clear, lo, pltpu.roll(hi, stride, 1))
            arrays[i | bit] = jnp.where(clear, pltpu.roll(lo, LANES - stride, 1), hi)
        bit *= 2
    return arrays


def partner(v, stride):
    real = (lane_of(v.shape) & stride) == 0
    if stride == 64:
        return pltpu.roll(v, 64, 1), real
    return jnp.where(real, pltpu.roll(v, LANES - stride, 1), pltpu.roll(v, stride, 1)), real


def times_minus_i(v, stride):
    other, real = partner(v, stride)
    return jnp.where(real, other, -other)


def times_plus_i(v, stride):
    other, real = partner(v, stride)
    return jnp.where(real, -other, other)


def z_modes(even, odd, w_ref):
    modes = dot(even, w_ref[0:NZ, :]) + dot(odd, w_ref[NZ : 2 * NZ, :])
    modes = modes * (1.0 / math.sqrt(NZ))
    return [modes[i : i + ROWS] for i in range(0, modes.shape[0], ROWS)]


def expand_pointwise(pw):
    group = lax.broadcasted_iota(jnp.int32, (256, C), 0) // 16
    member = lax.broadcasted_iota(jnp.int32, (256, C), 1)
    one_hot = (group == member).astype(BF)
    wide = dot_t(dot_t(one_hot, pw).astype(BF), one_hot)
    r = lax.broadcasted_iota(jnp.int32, (256, 256), 0) % 16
    s = lax.broadcasted_iota(jnp.int32, (256, 256), 1) % 16
    return jnp.where(r == s, wide, 0.0).astype(BF)


def k1(field_ref, w_ref, pw_ref, out_ref, kron_ref, x_ref, t_ref, p_ref, sems):
    table = pltpu.make_async_copy(w_ref, t_ref, sems.at[8])
    table.start()
    copies = []
    for n in range(4):
        for h in range(2):
            part = pl.ds(8 * h + 2 * n, 2)
            copies.append(pltpu.make_async_copy(field_ref.at[part], x_ref.at[part], sems.at[2 * n + h]))
            copies[-1].start()
    small = pltpu.make_async_copy(pw_ref, p_ref, sems.at[9])
    small.start()
    small.wait()
    kron_ref[...] = expand_pointwise(p_ref[...])
    table.wait()
    modes = []
    for n in range(4):
        copies[2 * n].wait()
        copies[2 * n + 1].wait()
        even = x_ref[2 * n : 2 * n + 2].reshape(2 * ROWS, NZ)
        odd = x_ref[8 + 2 * n : 10 + 2 * n].reshape(2 * ROWS, NZ)
        modes += z_modes(even, odd, t_ref)
    for p, v in enumerate(exchange(modes, 1)):
        out_ref[p] = v.astype(BF)


def y_transform(full, ty_ref, stride):
    out = []
    for x in range(full.shape[1] // YL):
        rows = jnp.concatenate([full[p, YL * x : YL * x + YL, :] for p in range(GY)], 0).astype(BF)
        t = dot(ty_ref[...], rows)
        cos, sin = t[0:48] + t[48:96], t[96:144] + t[144:192]
        out.append(cos + times_minus_i(sin, stride))
    return out


def ky_of(value, quarter):
    t = value + OWNED * quarter
    return t - jnp.where(t >= 48, 48, 0) - jnp.where(t >= 96, 48, 0)


def place():
    return 2 * lax.axis_index("chip") + lax.axis_index("core")


def first_of(member):
    return 32 * (member % 2) + member // 2


def k2(in_ref, spec_ref, ty_ref, out_ref, scratch):
    for x, v in enumerate(y_transform(in_ref[...].astype(F32), ty_ref, 16)):
        parts = [v[0:16], v[16:32], v[32:48], jnp.zeros((16, LANES), F32)]
        for b, part in enumerate(exchange(parts, 32)):
            scratch[pl.ds(16 * first_of(b) + x, 16, stride=32), :] = part
    quarter = place() % 4
    row = lax.broadcasted_iota(jnp.int32, (MY, OWNED), 0)
    mode = ky_of(lax.broadcasted_iota(jnp.int32, (MY, OWNED), 1), quarter)
    select = (mode == 3 * (row % 16) + row // 16).astype(BF)
    for b in range(KZL):
        moved = dot_t(select, spec_ref[pl.ds(b, 4 * LANES, stride=KZL), :].astype(BF))
        for k in range(4):
            for i in range(3):
                part = moved[16 * i : 16 * i + 16, LANES * k : LANES * k + LANES]
                scratch[pl.ds(16 * first_of(b) + 4 + 4 * i + k, 16, stride=32), :] = part
    out_ref[...] = scratch[...].astype(BF)


def fold(arrays):
    lane = lane_of(arrays[0].shape)
    zero = jnp.zeros_like(arrays[0])
    arrays = arrays + [zero, zero]
    for stride in (64, 32, 16):
        n = len(arrays) // 2
        clear = (lane & stride) == 0
        merged = []
        for lo, hi in zip(arrays[:n], arrays[n:]):
            moved = jnp.where(clear, hi, lo)
            back = pltpu.roll(moved, stride, 1)
            if stride < 64:
                back = jnp.where(clear, pltpu.roll(moved, LANES - stride, 1), back)
            merged.append(jnp.where(clear, lo, hi) + back)
        arrays = merged
    return arrays[0]


def k3(in_ref, tx_ref, e_ref, tinv_ref, out_ref, scratch):
    a = place() // 4
    scratch[...] = in_ref[...].astype(F32)
    data = jnp.concatenate([scratch[pl.ds(x, GX, stride=16), :] for x in range(XL)], 0).astype(BF)
    t = dot(tx_ref[...], data)
    fwd = t[0:48] + t[48:96] + times_minus_i(t[96:144] + t[144:192], 16)
    fwd = fwd.astype(BF)
    source = (
        jnp.where(a >= 12, 1, 0),
        1 + jnp.where(a >= 8, 1, 0),
        2 + jnp.where(a >= 4, 1, 0),
    )

    def weights(i, k):
        at = 4 + 4 * i + k
        return jnp.concatenate(
            [scratch[pl.ds(16 * first_of(source[r]) + at, 16, stride=32), :] for r in range(3)], 0
        )

    sums = []
    for i in range(3):
        real, imag = 0.0, 0.0
        for h in range(2):
            at = 256 * (2 * i + h)
            wide = dot(fwd, e_ref[:, at : at + 256])
            fr, fi = wide[:, 0:128], wide[:, 128:256]
            wr, wi = weights(i, h), weights(i, 2 + h)
            real += wr * fr - wi * fi
            imag += wr * fi + wi * fr
        sums += [real, imag]
    mixed = fold(sums)
    mixed = mixed.astype(BF)
    turned = times_plus_i(mixed.astype(F32), 16).astype(BF)
    moved = [
        jnp.where(lane_of(fwd.shape) >= 96, pltpu.roll(fwd.astype(F32), 96 - 32 * i, 1), 0.0)
        for i in range(3)
    ]
    moved = jnp.concatenate(moved, 0).astype(BF)
    row = lax.broadcasted_iota(jnp.int32, (NX, 3 * MX), 0)
    col = lax.broadcasted_iota(jnp.int32, (NX, 3 * MX), 1)
    owner = 2 * (row // 4 % 32) + row // 128
    quarter = owner % 4
    back_one = jnp.where(quarter == 1, jnp.where(a >= 12, 1, 0), 0)
    back_one += jnp.where(quarter == 2, jnp.where(a >= 8, 1, 0), 0)
    r = jnp.minimum(quarter, 2) - back_one
    wanted = MX * (row % 4) + 16 * r + owner // 4
    select = (col == wanted).astype(BF)
    result = dot(tinv_ref[...], jnp.concatenate([mixed, mixed, turned, turned], 0))
    result += dot(select, moved)
    out_ref[...] = result.astype(BF)


def k4(in_ref, ty_ref, out_ref, fwd_ref, scratch):
    scratch[...] = in_ref[...].astype(F32)
    for x in range(XL):
        parts = [scratch[pl.ds(4 * first_of(b) + x, 16, stride=8), :] for b in range(KZL)]
        parts = exchange(parts, 32)
        if x < 3:
            fwd_ref[16 * x : 16 * x + 16, :] = parts[3]
        v = jnp.concatenate(parts[0:3], 0)
        b = v.astype(BF)
        s = times_plus_i(v, 16).astype(BF)
        w = dot(ty_ref[...], jnp.concatenate([b, b, s, s], 0))
        for p in range(GY):
            out_ref[p, YL * x : YL * x + YL, :] = w[YL * p : YL * p + YL].astype(BF)


def slope(pre):
    square = pre * pre
    t = jnp.tanh(pre * (0.7978845608 + 0.7978845608 * 0.044715 * square))
    ramp = pre * (0.5 * 0.7978845608 + 1.5 * 0.7978845608 * 0.044715 * square)
    return (0.5 + 0.5 * t) + (1.0 - t * t) * ramp


def k5(waves_ref, field_ref, cot_ref, kron, w_ref, zt_ref, out_ref, grad):
    for n in range(ROWS // 16):
        rows = slice(16 * n, 16 * n + 16)
        parts = exchange([waves_ref[p, rows, :].astype(F32) for p in range(GY)], 1)
        waves = jnp.concatenate(parts, 0).astype(BF)
        x = field_ref[:, rows, :].reshape(C * 16, NZ)
        mapped = dot(kron[...], x)
        for h in range(2):
            pre = dot(waves, zt_ref[:, NZ * h : NZ * h + NZ]) + mapped[128 * h : 128 * h + 128]
            cot = cot_ref[8 * h : 8 * h + 8, rows, :].reshape(128, NZ).astype(F32)
            grad[8 * h : 8 * h + 8, rows, :] = (cot * slope(pre)).astype(BF).reshape(8, 16, NZ)
    even = grad[0:8].reshape(8 * ROWS, NZ)
    odd = grad[8:16].reshape(8 * ROWS, NZ)
    for p, v in enumerate(exchange(z_modes(even, odd, w_ref), 4)):
        for core, part in enumerate(exchange([v[0:48], v[48:96]], 64)):
            out_ref[8 * core + p] = part.astype(BF)


def k6(in_ref, ty_ref, near_ref, turn_ref, chip_ref, out_ref, factors):
    kx = lax.broadcasted_iota(jnp.int32, (MX, 96), 0)
    member = lax.broadcasted_iota(jnp.int32, (MX, 96), 1) % 32
    one_hot = (member == (kx * lax.axis_index("chip")) % 32).astype(BF)
    chip = dot(one_hot, chip_ref[...])
    for kx in range(MX):
        rows = slice(8 * kx, 8 * kx + 8)
        cos, sin = chip[kx : kx + 1, 0:128], chip[kx : kx + 1, 128:256]
        factors[rows, :] = near_ref[rows, :] * cos + turn_ref[rows, :] * sin
    full = in_ref[...].astype(F32)
    values = []
    for core in range(2):
        values += y_transform(full[8 * core : 8 * core + 8], ty_ref, 32)
    turned = [times_minus_i(v, 32) for v in values]
    low = lane_of((24, LANES)) < 64

    terms = values + turned
    for kx in range(0, MX, 2):
        rows = []
        for at in (8 * kx, 8 * kx + 8):
            acc = terms[0] * factors[at : at + 1, :]
            for n in range(1, 8):
                acc += terms[n] * factors[at + n : at + n + 1, :]
            even, odd = acc[0:24], acc[24:48]
            rows.append(jnp.where(low, even, odd) + pltpu.roll(jnp.where(low, odd, even), 64, 1))
        out_ref[24 * kx : 24 * kx + 48, :] = jnp.concatenate(rows, 0).astype(BF)


def k7(in_ref, fwd_ref, reorder_ref, spec_ref, mom_ref, out_ref, scratch, result, sems):
    quarter = place() % 4
    total = in_ref[0:72, :].astype(F32)
    for g in range(1, 16):
        total += in_ref[72 * g : 72 * g + 72, :].astype(F32)
    scratch[0:72, :] = total
    scratch[72:80, :] = jnp.zeros((8, LANES), F32)
    total = scratch[0:40, :] + scratch[36:76, :]
    row = lax.broadcasted_iota(jnp.int32, (2 * LANES, 120), 0)
    col = lax.broadcasted_iota(jnp.int32, (2 * LANES, 120), 1) % 40
    mode = row % LANES
    select = ((col == 18 * (row // LANES) + mode // 2) & (mode < OWNED)).astype(BF)
    parts = []
    for _ in range(3):
        parts.append(total.astype(BF).astype(F32))
        total = total - parts[-1]
    moved = dot(select, jnp.concatenate(parts, 0).astype(BF))
    first, second = moved[0:LANES], moved[LANES : 2 * LANES]
    odd = lax.broadcasted_iota(jnp.int32, (LANES, LANES), 0) % 2
    upper = lane_of((LANES, LANES)) // 64
    grads = jnp.where(upper == 0, first, second)
    other = jnp.where(upper == 0, pltpu.roll(first, 64, 1), pltpu.roll(second, 64, 1))
    grads = jnp.where(upper == odd, grads, other)
    row = lax.broadcasted_iota(jnp.int32, (LANES, MY), 0)
    col = lax.broadcasted_iota(jnp.int32, (LANES, MY), 1)
    hit = (ky_of(row, quarter) == 3 * (col % 16) + col // 16) & (row < OWNED)
    fwd = dot(hit.astype(BF), fwd_ref[...].astype(BF)).astype(BF)
    fwd = dot(fwd, reorder_ref[...])
    grads = grads.T[:, 0:OWNED]
    fwd = fwd.T[:, 0:OWNED]
    grad_r = jnp.concatenate([grads[0:32], grads[64:96]], 0)
    grad_i = jnp.concatenate([grads[32:64], grads[96:128]], 0)
    copies = []
    for c in range(C):
        fr = fwd[4 * c : 4 * c + 4]
        fi = fwd[64 + 4 * c : 68 + 4 * c]
        fr = jnp.concatenate([fr] * 16, 0)
        fi = jnp.concatenate([fi] * 16, 0)
        d_real = grad_r * fr + grad_i * fi
        d_imag = grad_i * fr - grad_r * fi
        result[0, c] = mom_ref[0, c] - 0.25 * (d_real + 2.0 * C * spec_ref[0, c])
        result[1, c] = mom_ref[1, c] - 0.25 * (d_imag + 2.0 * C * spec_ref[1, c])
        if c % 4 == 3:
            for r in range(2):
                part = pl.ds(c - 3, 4)
                copy = pltpu.make_async_copy(
                    result.at[r, part], out_ref.at[r, part], sems.at[2 * (c // 4) + r]
                )
                copy.start()
                copies.append(copy)
    for copy in copies:
        copy.wait()


def call(body, out, *args, scratch=(), hbm=(), out_space=pltpu.VMEM):
    specs = [
        pl.BlockSpec(memory_space=pltpu.HBM if i in hbm else pltpu.VMEM) for i in range(len(args))
    ]
    out_spec = pl.BlockSpec(memory_space=out_space)
    return pl.pallas_call(
        body,
        out_shape=out,
        in_specs=specs,
        out_specs=jax.tree.map(lambda _: out_spec, out),
        scratch_shapes=list(scratch),
        compiler_params=pltpu.CompilerParams(vmem_limit_bytes=40 * 1024 * 1024),
    )(*args)


def swap(value, axis):
    return lax.all_to_all(value, axis, split_axis=0, concat_axis=0, tiled=True)


def on_device(field, pointwise, spectral, momentum, cotangent):
    field = field.reshape(C, ROWS, NZ)
    cotangent = cotangent.reshape(C, ROWS, NZ)
    spectral = jnp.transpose(spectral, (1, 2, 3, 4, 0))
    momentum = jnp.transpose(momentum, (1, 2, 3, 4, 0))
    z_mid, z_half, z_inv = [jnp.asarray(t) for t in z_tables()]
    zshape = jax.ShapeDtypeStruct((GY, ROWS, LANES), BF)

    zmodes, kron = call(
        k1,
        (zshape, jax.ShapeDtypeStruct((256, 256), BF)),
        pltpu.with_memory_space_constraint(field, pltpu.HBM),
        pltpu.with_memory_space_constraint(z_mid, pltpu.HBM),
        pltpu.with_memory_space_constraint(pointwise, pltpu.HBM),
        hbm=(0, 1, 2),
        scratch=[
            pltpu.VMEM((C, ROWS, NZ), BF),
            pltpu.VMEM((2 * NZ, LANES), BF),
            pltpu.VMEM((C, C), BF),
            pltpu.SemaphoreType.DMA((10,)),
        ],
    )
    zmodes = swap(zmodes, "gy")
    sent = call(
        k2,
        jax.ShapeDtypeStruct((GX * 16, LANES), BF),
        zmodes,
        spectral.reshape(2 * C * C * KZL, OWNED),
        jnp.asarray(y_forward_table(TRIPLES)),
        scratch=[pltpu.VMEM((GX * 16, LANES), F32)],
    )
    got = swap(sent.reshape(GX, 16, LANES), CORE_FIRST).reshape(GX * 16, LANES)
    sent = call(
        k3,
        jax.ShapeDtypeStruct((NX, LANES), BF),
        got,
        jnp.asarray(x_forward_table()),
        jnp.asarray(expand_table()),
        jnp.asarray(x_inverse_table()),
        scratch=[pltpu.VMEM((GX * 16, LANES), F32)],
    )
    back = swap(sent.reshape(GX, XL, LANES), CORE_FIRST).reshape(NX, LANES)
    waves, fwd = call(
        k4,
        (zshape, jax.ShapeDtypeStruct((MY, LANES), F32)),
        back,
        jnp.asarray(y_inverse_table()),
        scratch=[pltpu.VMEM((NX, LANES), F32)],
    )
    zgrads = call(
        k5,
        jax.ShapeDtypeStruct((2 * GY, ROWS // 2, LANES), BF),
        swap(waves, "gy"),
        field,
        cotangent,
        kron,
        z_half,
        z_inv,
        scratch=[pltpu.VMEM((C, ROWS, NZ), BF)],
    )
    partial = call(
        k6,
        jax.ShapeDtypeStruct((MX * MY // 2, LANES), BF),
        swap(zgrads, ("core", "gy")),
        jnp.asarray(y_forward_table(PAIRS)),
        *[jnp.asarray(t) for t in partial_tables()],
        scratch=[pltpu.VMEM((8 * MX, LANES), F32)],
    )
    partial = swap(partial.reshape(GX, OWNED // 4, 2, LANES), GXS).reshape(MX * MY // 2, LANES)
    result = call(
        k7,
        jax.ShapeDtypeStruct((2, C, C * KZL, OWNED), F32),
        partial,
        fwd,
        jnp.asarray(reorder_table()),
        spectral.reshape(2, C, C * KZL, OWNED),
        momentum.reshape(2, C, C * KZL, OWNED),
        scratch=[
            pltpu.VMEM((80, LANES), F32),
            pltpu.VMEM((2, C, C * KZL, OWNED), F32),
            pltpu.SemaphoreType.DMA((8,)),
        ],
        out_space=pltpu.HBM,
    )
    result = result.reshape(2, C, C, KZL, OWNED)
    return jnp.transpose(result, (4, 0, 1, 2, 3))


def solution(mesh):
    chips = jax.sharding.Mesh(mesh.devices.reshape(GX // 2, 2, GY), ("chip", "core", "gy"))
    in_specs = (
        P(None, GXS, "gy", None),
        P(),
        P(GXS, None, None, None, "gy"),
        P(GXS, None, None, None, "gy"),
        P(None, GXS, "gy", None),
    )
    out_specs = P(GXS, None, None, None, "gy")
    return jax.shard_map(
        on_device, mesh=chips, in_specs=in_specs, out_specs=out_specs, check_vma=False
    )
```
